32 devices in a mesh: phase: 4 (over y, x), slab: 8 (over z, core).
Axes of the slice: x: 2, y: 2, z: 4, core: 2. Of those that a mesh axis runs over, the one named last changes fastest.
Arguments:
- pressure: float32 [2, 16, 32, 24576], P(None, 'phase', None, 'slab'), may hold values from -6 to 6
- mode_shapes: float32 [1024, 24576], P('phase', 'slab'), may hold values from -0.0546875 to 0.0546875
- point_weight: float32 [24576], P('slab'), may hold values from 0.5 to 2
- panel_order: int32 [8], replicated, may hold values from 0 to 7, each once
Outputs:
- influence: float32 [2, 16, 32, 1024], P(None, None, 'phase', 'slab')
The draws below stay inside these ranges and needn't reach their ends.
Inputs may be any that keep to these rules, and one draw needn't show every extreme that they name: panel_order names each of 0 to 7 once.
All inputs are finite; a program needn't handle non-finite values.
Results may differ from the reference program's by a relative error of at most 0.00007.
Values sent between devices are 32-bit elements; how exact they have to be, the bound alone decides.
A program may use at most 64 MiB of HBM per device.

```python
import math
import jax
import jax.numpy as jnp
from jax import lax

NB = 16
J = 32
S = 24576
MODES = 1024
PANEL = 128
NPANEL = 8


def raised(array, rng, source, target, blocks, factor):
    def block_of(axis_at):
        return (jnp.arange(array.shape[axis_at]) // (array.shape[axis_at] // blocks)).reshape((-1,) + (1,) * (array.ndim - 1 - axis_at))

    near = jax.random.permutation(rng, blocks)[block_of(target)]
    far = (block_of(target) + blocks // 2) % blocks
    return jnp.where((block_of(source) == near) | (block_of(source) == far), factor * array, array)


def levels(stream_key, shape, split, low, largest):
    def one(axis_at, blocks):
        heights = jax.random.uniform(jax.random.fold_in(jax.random.fold_in(stream_key, 6), axis_at), (blocks,), jnp.float32, low / len(split), largest / len(split))
        return jnp.repeat(jnp.exp(heights), shape[axis_at] // blocks).reshape((-1,) + (1,) * (len(shape) - axis_at - 1))

    gain = one(*split[0])
    for cut in split[1:]:
        gain = gain * one(*cut)
    return gain


def centred(stream_key, shape, scale, reach, cuts=(), held_as=jnp.bfloat16):
    array = scale * jax.random.normal(stream_key, shape, jnp.float32)
    if cuts:
        array = array * levels(stream_key, shape, cuts, -0.22, 0.18)
    return jnp.clip(array, -reach, reach).astype(held_as)


def noise_with(stream_key, dims, width, limit, pieces, heavy, held_as=jnp.bfloat16):
    drawn = width * jax.random.normal(stream_key, dims, jnp.float32)
    if pieces:
        drawn = drawn * levels(stream_key, dims, pieces, -0.22, 0.18)
    return jnp.clip(raised(drawn, jax.random.fold_in(stream_key, 3), *heavy), -limit, limit).astype(held_as)


def setup_inputs(seed: int = 0) -> dict:
    key_list = jax.random.split(jax.random.key(seed), 5)
    pressure = centred(key_list[0], (2, NB, J, S), 1.0, 6.0, ((1, 4), (3, 8)), jnp.float32)
    mode_shapes = noise_with(key_list[1], (MODES, S), S ** -0.5, 0.0546875, ((0, 4), (1, 8)), (1, 0, 8, 2.0), jnp.float32)
    point_weight = jnp.clip(jnp.exp(math.log(2.0) - 1.3862944 * jax.random.uniform(key_list[2], (S,), jnp.float32) ** levels(key_list[2], (S,), ((0, 8),), -0.2, 0.2)), 0.5, 2.0)
    panel_order = jax.random.permutation(key_list[3], NPANEL).astype(jnp.int32)
    return {"pressure": pressure, "mode_shapes": mode_shapes, "point_weight": point_weight, "panel_order": panel_order}


def blade_table(blades):
    phases = jnp.arange(blades, dtype=jnp.int32)
    index = phases[None, :] * phases[:, None] % blades
    theta = index.astype(jnp.float32) * (2.0 * math.pi / blades)
    cosine = jnp.cos(theta)
    sine = jnp.sin(theta)
    upper = jnp.concatenate([cosine, -sine], axis=1)
    lower = jnp.concatenate([sine, cosine], axis=1)
    return jnp.concatenate([upper, lower], axis=0) * (1.0 / math.sqrt(blades))

def reference(pressure, mode_shapes, point_weight, panel_order):
    weighted = mode_shapes * point_weight[None, :]
    rows = pressure.reshape(2 * NB * J, S)
    forces = lax.dot_general(rows, weighted, (((1,), (1,)), ((), ())), precision=lax.Precision.HIGHEST, preferred_element_type=jnp.float32)
    panels = forces.reshape(2 * NB * J, NPANEL, PANEL)
    reordered = jnp.take(panels, panel_order.astype(jnp.int32), axis=1).reshape(2 * NB, J * MODES)
    table = blade_table(NB)
    result = jnp.dot(table, reordered, precision=lax.Precision.HIGHEST, preferred_element_type=jnp.float32)
    return result.reshape(2, NB, J, MODES)
```

```python
import math

import jax
import jax.numpy as jnp
from jax import lax
from jax.experimental import pallas as pl
from jax.experimental.pallas import tpu as pltpu
from jax.sharding import PartitionSpec as P

MESH = pl.DeviceIdType.MESH
F32 = jnp.float32
BF16 = jnp.bfloat16
SLABS = 8
CHUNKS = 4
OWN, REM = 0, 1


def blade_table(blades, count):
    phases = jnp.arange(count, dtype=jnp.int32)
    target = jnp.arange(blades, dtype=jnp.int32)
    index = target[:, None] * phases[None, :] % blades
    theta = index.astype(jnp.float32) * (2.0 * math.pi / blades)
    cosine = jnp.cos(theta)
    sine = jnp.sin(theta)
    upper = jnp.concatenate([cosine, -sine], axis=1)
    lower = jnp.concatenate([sine, cosine], axis=1)
    return jnp.concatenate([upper, lower], axis=0) * (1.0 / math.sqrt(blades))


def general(pressure, mode_shapes, point_weight, panel_order):
    weighted = mode_shapes * point_weight[None, :]
    phase_dev = pressure.shape[1]
    excite = pressure.shape[2]
    rows = pressure.reshape(2 * phase_dev * excite, pressure.shape[3])
    partial_forces = lax.dot_general(
        rows,
        lax.all_gather(weighted, "phase", axis=0, tiled=True),
        (((1,), (1,)), ((), ())),
        precision=lax.Precision.HIGHEST,
        preferred_element_type=jnp.float32,
    )
    row_count = partial_forces.shape[0]
    panel_count = panel_order.shape[0]
    panels = partial_forces.reshape(row_count, panel_count, -1)
    selector = (panel_order[:, None] == jnp.arange(panel_count, dtype=jnp.int32)[None, :]).astype(
        jnp.float32
    )
    reordered = jnp.einsum(
        "rqc,pq->rpc", panels, selector, precision=lax.Precision.HIGHEST
    ).reshape(row_count, -1)
    slab_count = lax.axis_size("slab")
    total = lax.psum(reordered, "slab")
    keep_width = total.shape[1] // slab_count
    share = lax.dynamic_slice_in_dim(total, lax.axis_index("slab") * keep_width, keep_width, 1)
    mode_local = share.shape[1]
    forces = share.reshape(2, phase_dev, excite, mode_local)
    blades = phase_dev * lax.axis_size("phase")
    gathered = lax.all_to_all(forces, "phase", split_axis=2, concat_axis=1, tiled=True)
    table = blade_table(blades, blades)
    result = jnp.dot(
        table,
        gathered.reshape(2 * blades, -1),
        precision=lax.Precision.HIGHEST,
        preferred_element_type=jnp.float32,
    )
    result = result.reshape(2, blades, -1, mode_local)
    return result


def split(value):
    high = value.astype(BF16)
    return high, (value - high.astype(F32)).astype(BF16)


def product(a_high, a_low, b_high, b_low):
    def dot(a, b):
        return lax.dot_general(a, b, (((1,), (1,)), ((), ())), preferred_element_type=F32)

    return dot(a_high, b_high) + dot(a_high, b_low) + dot(a_low, b_high)


PIECES = {
    OWN: ((0, 2, 0, 4), (2, 1, 0, 4), (3, 1, 0, 4)),
    REM: ((0, 3, 0, 2), (0, 3, 2, 1), (0, 3, 3, 1), (3, 1, 0, 4)),
}


def kernel(
    index_ref, a_hbm, b_hbm, w_ref, out_ref,
    a_own, b_own, a_rem, b_rem, a_hi, a_lo, b_hi, b_lo, part, parts, red, plane, picked, gathered,
    load_sem, a_send, a_recv, b_send, b_recv, r_send, r_recv, p_send, p_recv, g_send, g_recv,
):
    p = lax.axis_index("phase")
    d = lax.axis_index("slab")
    x, y = p % 2, p // 2
    x_near = y * 2 + (1 - x)
    y_near = (1 - y) * 2 + x

    loads = [
        pltpu.make_async_copy(a_hbm.at[:, :, pl.ds(8 * g, 8), :], a_own.at[g], load_sem.at[g])
        for g in range(CHUNKS)
    ]
    loads.append(pltpu.make_async_copy(b_hbm, b_own, load_sem.at[CHUNKS]))
    for load in loads:
        load.start()

    barrier = pltpu.get_barrier_semaphore()
    for o in range(1, 4):
        pl.semaphore_signal(
            barrier, inc=1, device_id={"phase": (p + o) % 4, "slab": d}, device_id_type=MESH
        )
    for o in range(1, SLABS):
        pl.semaphore_signal(
            barrier, inc=1, device_id={"phase": p, "slab": (d + o) % SLABS}, device_id_type=MESH
        )
    pl.semaphore_wait(barrier, 3 + SLABS - 1)

    def a_copy(t):
        return pltpu.make_async_remote_copy(
            src_ref=a_hbm.at[:, :, pl.ds(8 * t, 8), :], dst_ref=a_rem.at[t],
            send_sem=a_send.at[t], recv_sem=a_recv.at[t],
            device_id={"phase": x_near, "slab": d}, device_id_type=MESH,
        )

    def b_copy(t):
        return pltpu.make_async_remote_copy(
            src_ref=b_hbm.at[pl.ds(64 * t, 64)], dst_ref=b_rem.at[pl.ds(64 * t, 64)],
            send_sem=b_send.at[t], recv_sem=b_recv.at[t],
            device_id={"phase": y_near, "slab": d}, device_id_type=MESH,
        )

    def piece(kind, i, kk, act):
        slot, slots, group, groups = PIECES[kind][i]
        peer = ((kind + x) % 2) * 4 + kk
        where = (pl.ds(slot, slots), pl.ds(group, groups))

        @pl.when(peer != d)
        def _():
            act(pltpu.make_async_remote_copy(
                src_ref=part.at[(kind * 4 + kk,) + where], dst_ref=parts.at[(d,) + where],
                send_sem=r_send.at[i, kind * 4 + kk], recv_sem=r_recv.at[i, d],
                device_id={"phase": p, "slab": peer}, device_id_type=MESH,
            ))

    def send(kind, i):
        for kk in range(4):
            piece(kind, i, kk, lambda copy: copy.start())

    def split_a(source, g, kind):
        high, low = split(source[g].reshape(64, -1))
        rows = pl.ds(kind * 256 + 64 * g, 64)
        a_hi[rows], a_lo[rows] = high, low

    def split_b(source, t, kind):
        high, low = split(source[pl.ds(64 * t, 64)] * w_ref[...])
        rows = pl.ds(kind * 256 + 64 * t, 64)
        b_hi[rows], b_lo[rows] = high, low

    def block(kind, group, groups, slot, slots):
        rows = pl.ds(kind * 256 + 64 * group, 64 * groups)
        cols = pl.ds(128 * slot, 128 * slots)
        value = product(a_hi[rows], a_lo[rows], b_hi[cols], b_lo[cols])
        value = value.reshape(groups, 2, 4, 8, 128 * slots)
        for kk in range(4):
            for s in range(slots):
                part[kind * 4 + kk, slot + s, pl.ds(group, groups)] = (
                    value[:, :, kk, :, 128 * s:128 * (s + 1)]
                )

    for t in range(2):
        a_copy(t).start()
        b_copy(t).start()

    for load in loads:
        load.wait()
    for t in range(CHUNKS):
        split_a(a_own, t, OWN)
        split_b(b_own, t, OWN)
    block(OWN, 0, 4, 0, 2)
    send(OWN, 0)

    for t in range(CHUNKS):
        a_copy(t).wait()
        if t + 2 < CHUNKS:
            a_copy(t + 2).start()
        b_copy(t).wait()
        if t + 2 < CHUNKS:
            b_copy(t + 2).start()
        split_a(a_rem, t, REM)
        split_b(b_rem, t, REM)
        if t == 1:
            block(REM, 0, 2, 0, 3)
            send(REM, 0)
            block(OWN, 0, 4, 2, 1)
            send(OWN, 1)
        if t == 2:
            block(REM, 2, 1, 0, 3)
            send(REM, 1)
        if t == 3:
            block(REM, 3, 1, 0, 3)
            send(REM, 2)
            block(REM, 0, 4, 3, 1)
            send(REM, 3)
            block(OWN, 0, 4, 3, 1)
            send(OWN, 2)

    mine = (d // 4 + x) % 2
    for kind in (OWN, REM):
        @pl.when(mine == kind)
        def _():
            for i, (slot, slots, group, groups) in enumerate(PIECES[kind]):
                for o in range(1, SLABS):
                    other = (d + o) % SLABS
                    landed = parts.at[other, pl.ds(slot, slots), pl.ds(group, groups)]
                    pltpu.make_async_copy(landed, landed, r_recv.at[i, other]).wait()

    total = part[mine * 4 + d % 4]
    for o in range(1, SLABS):
        total = total + parts[(d + o) % SLABS]
    red[...] = total

    def plane_copy(o):
        peer = (p + o) % 4
        return pltpu.make_async_remote_copy(
            src_ref=red.at[:, peer], dst_ref=plane.at[pl.ds(4 * p, 4)],
            send_sem=p_send.at[o], recv_sem=p_recv.at[p],
            device_id={"phase": peer, "slab": d}, device_id_type=MESH,
        )

    for o in range(1, 4):
        plane_copy(o).start()
    plane[pl.ds(4 * p, 4)] = red[:, p]
    for o in range(1, 4):
        other = (p + o) % 4
        landed = plane.at[pl.ds(4 * other, 4)]
        pltpu.make_async_copy(landed, landed, p_recv.at[other]).wait()

    def slab_copy(o):
        peer = (d + o) % SLABS
        return pltpu.make_async_remote_copy(
            src_ref=picked.at[o], dst_ref=gathered.at[d],
            send_sem=g_send.at[o], recv_sem=g_recv.at[d],
            device_id={"phase": p, "slab": peer}, device_id_type=MESH,
        )

    for o in range(1, SLABS):
        peer = (d + o) % SLABS
        for half in range(2):
            picked[o, half] = plane[index_ref[half * SLABS + peer]]
        slab_copy(o).start()
    for half in range(2):
        gathered[d, half] = plane[index_ref[half * SLABS + d]]
    for o in range(1, SLABS):
        other = (d + o) % SLABS
        landed = gathered.at[other]
        pltpu.make_async_copy(landed, landed, g_recv.at[other]).wait()

    blades = 16
    scale = 1.0 / math.sqrt(blades)
    cosine = [round(math.cos(2 * math.pi * i / blades), 15) * scale for i in range(blades)]
    sine = [round(math.sin(2 * math.pi * i / blades), 15) * scale for i in range(blades)]
    for b in range(blades):
        real, imag = None, None
        for k in range(blades):
            c, s = cosine[k * b % blades], sine[k * b % blades]
            re, im = gathered[k % 8, k // 8, 0], gathered[k % 8, k // 8, 1]
            for sign, coef, u, v in ((-1.0, c, re, im), (1.0, s, im, re)):
                if coef == 0.0:
                    continue
                first = u * (coef if sign < 0 else -coef)
                second = v * coef
                real = first if real is None else real + first
                imag = second if imag is None else imag + second
        out_ref[0, b] = real
        out_ref[1, b] = imag

    for kind in (OWN, REM):
        for i in range(len(PIECES[kind])):
            for kk in range(4):
                piece(kind, i, kk, lambda copy: copy.wait_send())
    for o in range(1, 4):
        plane_copy(o).wait_send()
    for o in range(1, SLABS):
        slab_copy(o).wait_send()


def fused(pressure, mode_shapes, point_weight, panel_order):
    points = pressure.shape[3]
    owner = panel_order // 2
    half = jnp.arange(2, dtype=jnp.int32)[:, None]
    far = (owner[None, :] // 2 != half).astype(jnp.int32)
    index = ((half * 2 + owner[None, :] % 2) * 4 + far * 2 + panel_order[None, :] % 2).reshape(-1)
    vmem = pltpu.VMEM
    dma = pltpu.SemaphoreType.DMA
    return pl.pallas_call(
        kernel,
        out_shape=jax.ShapeDtypeStruct((2, 16, 8, 128), F32),
        in_specs=[
            pl.BlockSpec(memory_space=pltpu.SMEM),
            pl.BlockSpec(memory_space=pl.ANY),
            pl.BlockSpec(memory_space=pl.ANY),
            pl.BlockSpec(memory_space=pltpu.VMEM),
        ],
        out_specs=pl.BlockSpec(memory_space=pltpu.VMEM),
        scratch_shapes=[
            vmem((4, 2, 4, 8, points), F32),
            vmem((256, points), F32),
            vmem((4, 2, 4, 8, points), F32),
            vmem((256, points), F32),
            vmem((512, points), BF16),
            vmem((512, points), BF16),
            vmem((512, points), BF16),
            vmem((512, points), BF16),
            vmem((8, 4, 4, 2, 8, 128), F32),
            vmem((8, 4, 4, 2, 8, 128), F32),
            vmem((4, 4, 2, 8, 128), F32),
            vmem((16, 2, 8, 128), F32),
            vmem((8, 2, 2, 8, 128), F32),
            vmem((8, 2, 2, 8, 128), F32),
            dma((5,)),
            dma((4,)), dma((4,)), dma((4,)), dma((4,)),
            dma((4, 8)), dma((4, 8)),
            dma((4,)), dma((4,)),
            dma((8,)), dma((8,)),
        ],
        compiler_params=pltpu.CompilerParams(
            collective_id=0, has_side_effects=True, vmem_limit_bytes=56 * 1024 * 1024
        ),
        cost_estimate=pl.CostEstimate(
            flops=6 * 512 * 512 * points, bytes_accessed=16 * 256 * points, transcendentals=0
        ),
    )(index, pressure, mode_shapes, point_weight.reshape(1, points))


def solution(mesh):
    def shards(pressure, mode_shapes, point_weight, panel_order):
        fits = (
            mesh.shape["phase"] == 4
            and mesh.shape["slab"] == SLABS
            and pressure.shape[:3] == (2, 4, 32)
            and pressure.shape[3] % 256 == 0
            and pressure.shape[3] <= 3072
            and mode_shapes.shape[0] == 256
            and panel_order.shape[0] == 8
        )
        body = fused if fits else general
        return body(pressure, mode_shapes, point_weight, panel_order)

    placed = (P(None, "phase", None, "slab"), P("phase", "slab"), P("slab"), P())
    return jax.shard_map(
        shards,
        mesh=mesh,
        in_specs=placed,
        out_specs=P(None, None, "phase", "slab"),
        check_vma=False,
    )
```

```python
import math

import jax
import jax.numpy as jnp
from jax import lax
from jax.experimental import pallas as pl
from jax.experimental.pallas import tpu as pltpu
from jax.sharding import PartitionSpec as P

MESH = pl.DeviceIdType.MESH
F32 = jnp.float32
BF16 = jnp.bfloat16
SLABS = 8
CHUNKS = 8
DEPTH = 3
OWN, REM = 0, 1


def blade_table(blades, count):
    phases = jnp.arange(count, dtype=jnp.int32)
    target = jnp.arange(blades, dtype=jnp.int32)
    index = target[:, None] * phases[None, :] % blades
    theta = index.astype(jnp.float32) * (2.0 * math.pi / blades)
    cosine = jnp.cos(theta)
    sine = jnp.sin(theta)
    upper = jnp.concatenate([cosine, -sine], axis=1)
    lower = jnp.concatenate([sine, cosine], axis=1)
    return jnp.concatenate([upper, lower], axis=0) * (1.0 / math.sqrt(blades))


def general(pressure, mode_shapes, point_weight, panel_order):
    weighted = mode_shapes * point_weight[None, :]
    phase_dev = pressure.shape[1]
    excite = pressure.shape[2]
    rows = pressure.reshape(2 * phase_dev * excite, pressure.shape[3])
    partial_forces = lax.dot_general(
        rows,
        lax.all_gather(weighted, "phase", axis=0, tiled=True),
        (((1,), (1,)), ((), ())),
        precision=lax.Precision.HIGHEST,
        preferred_element_type=jnp.float32,
    )
    row_count = partial_forces.shape[0]
    panel_count = panel_order.shape[0]
    panels = partial_forces.reshape(row_count, panel_count, -1)
    selector = (panel_order[:, None] == jnp.arange(panel_count, dtype=jnp.int32)[None, :]).astype(
        jnp.float32
    )
    reordered = jnp.einsum(
        "rqc,pq->rpc", panels, selector, precision=lax.Precision.HIGHEST
    ).reshape(row_count, -1)
    slab_count = lax.axis_size("slab")
    total = lax.psum(reordered, "slab")
    keep_width = total.shape[1] // slab_count
    share = lax.dynamic_slice_in_dim(total, lax.axis_index("slab") * keep_width, keep_width, 1)
    mode_local = share.shape[1]
    forces = share.reshape(2, phase_dev, excite, mode_local)
    blades = phase_dev * lax.axis_size("phase")
    gathered = lax.all_to_all(forces, "phase", split_axis=2, concat_axis=1, tiled=True)
    table = blade_table(blades, blades)
    result = jnp.dot(
        table,
        gathered.reshape(2 * blades, -1),
        precision=lax.Precision.HIGHEST,
        preferred_element_type=jnp.float32,
    )
    result = result.reshape(2, blades, -1, mode_local)
    return result


def split(value):
    high = value.astype(BF16)
    return high, (value - high.astype(F32)).astype(BF16)


def product(a_high, a_low, b_high, b_low):
    def dot(a, b):
        return lax.dot_general(a, b, (((1,), (1,)), ((), ())), preferred_element_type=F32)

    return dot(a_high, b_high) + dot(a_high, b_low) + dot(a_low, b_high)


PIECES = {
    OWN: ((0, 2, 0, 4), (2, 1, 0, 4), (3, 1, 0, 4)),
    REM: ((0, 3, 0, 2), (0, 3, 2, 1), (0, 3, 3, 1), (3, 1, 0, 4)),
}


def kernel(
    order_ref, a_hbm, b_hbm, w_ref, out_ref,
    a_own, b_own, a_rem, b_rem, a_hi, a_lo, b_hi, b_lo, part, sibling, chip, parts, red, plane, picked,
    gathered,
    load_sem, a_send, a_recv, b_send, b_recv, s_send, s_recv, r_send, r_recv, p_send, p_recv, g_send,
    g_recv,
):
    p = lax.axis_index("phase")
    d = lax.axis_index("slab")
    x, y = p % 2, p // 2
    z, core = d // 2, d % 2
    x_near = y * 2 + (1 - x)
    y_near = (1 - y) * 2 + x
    core_near = z * 2 + (1 - core)

    barrier = pltpu.get_barrier_semaphore()
    for o in range(1, 4):
        pl.semaphore_signal(
            barrier, inc=1, device_id={"phase": (p + o) % 4, "slab": d}, device_id_type=MESH
        )
    for o in range(1, SLABS):
        pl.semaphore_signal(
            barrier, inc=1, device_id={"phase": p, "slab": (d + o) % SLABS}, device_id_type=MESH
        )

    def a_chunk(t):
        return a_hbm.at[t % 2, :, pl.ds(8 * (t // 2), 8), :]

    loads = [pltpu.make_async_copy(a_chunk(t), a_own.at[t], load_sem.at[t]) for t in range(CHUNKS)]
    loads.append(pltpu.make_async_copy(b_hbm, b_own, load_sem.at[CHUNKS]))
    for load in loads:
        load.start()
    pl.semaphore_wait(barrier, 3 + SLABS - 1)

    def a_copy(t):
        return pltpu.make_async_remote_copy(
            src_ref=a_chunk(t), dst_ref=a_rem.at[t],
            send_sem=a_send.at[t], recv_sem=a_recv.at[t],
            device_id={"phase": x_near, "slab": d}, device_id_type=MESH,
        )

    def b_copy(t):
        return pltpu.make_async_remote_copy(
            src_ref=b_hbm.at[pl.ds(32 * t, 32)], dst_ref=b_rem.at[pl.ds(32 * t, 32)],
            send_sem=b_send.at[t], recv_sem=b_recv.at[t],
            device_id={"phase": y_near, "slab": d}, device_id_type=MESH,
        )

    def core_copy(kind, i):
        slot, slots, group, groups = PIECES[kind][i]
        where = (slice(None), pl.ds(slot, slots), pl.ds(group, groups))
        return pltpu.make_async_remote_copy(
            src_ref=part.at[(kind, 1 - core) + where], dst_ref=sibling.at[(kind,) + where],
            send_sem=s_send.at[kind, i], recv_sem=s_recv.at[kind, i],
            device_id={"phase": p, "slab": core_near}, device_id_type=MESH,
        )

    def peer_copy(kind, i, h, act):
        slot, slots, group, groups = PIECES[kind][i]
        peer_z = ((kind + x) % 2) * 2 + h
        where = (pl.ds(slot, slots), pl.ds(group, groups))

        @pl.when(peer_z != z)
        def _():
            act(pltpu.make_async_remote_copy(
                src_ref=chip.at[(kind, h) + where], dst_ref=parts.at[(z,) + where],
                send_sem=r_send.at[kind, i, h], recv_sem=r_recv.at[i, z],
                device_id={"phase": p, "slab": peer_z * 2 + core}, device_id_type=MESH,
            ))

    def forward(kind, i):
        core_copy(kind, i).wait()
        slot, slots, group, groups = PIECES[kind][i]
        for h in range(2):
            where = (h, pl.ds(slot, slots), pl.ds(group, groups))
            chip[(kind,) + where] = part[(kind, core) + where] + sibling[(kind,) + where]
            peer_copy(kind, i, h, lambda copy: copy.start())

    def split_a(source, t, kind):
        high, low = split(source[t].reshape(32, -1))
        rows = pl.ds(kind * 256 + 32 * t, 32)
        a_hi[rows], a_lo[rows] = high, low

    def split_b(source, t, kind):
        high, low = split(source[pl.ds(32 * t, 32)] * w_ref[...])
        rows = pl.ds(kind * 256 + 32 * t, 32)
        b_hi[rows], b_lo[rows] = high, low

    def block(kind, i):
        slot, slots, group, groups = PIECES[kind][i]
        rows = pl.ds(kind * 256 + 64 * group, 64 * groups)
        cols = pl.ds(128 * slot, 128 * slots)
        value = product(a_hi[rows], a_lo[rows], b_hi[cols], b_lo[cols])
        value = value.reshape(groups, 2, 4, 8, 128 * slots)
        for kk in range(4):
            for s in range(slots):
                part[kind, kk % 2, kk // 2, slot + s, pl.ds(group, groups)] = (
                    value[:, :, kk, :, 128 * s:128 * (s + 1)]
                )
        core_copy(kind, i).start()

    for t in range(DEPTH):
        a_copy(t).start()
        b_copy(t).start()

    for load in loads:
        load.wait()
    for t in range(CHUNKS):
        split_a(a_own, t, OWN)
        split_b(b_own, t, OWN)
    block(OWN, 0)

    for t in range(CHUNKS):
        b_copy(t).wait()
        if t + DEPTH < CHUNKS:
            b_copy(t + DEPTH).start()
        split_b(b_rem, t, REM)
        if t == 7:
            block(OWN, 2)
        a_copy(t).wait()
        if t + DEPTH < CHUNKS:
            a_copy(t + DEPTH).start()
        split_a(a_rem, t, REM)
        if t == 0:
            forward(OWN, 0)
        if t == 3:
            block(REM, 0)
            block(OWN, 1)
        if t == 4:
            forward(REM, 0)
            forward(OWN, 1)
        if t == 5:
            block(REM, 1)
        if t == 6:
            forward(REM, 1)
        if t == 7:
            block(REM, 3)
            forward(OWN, 2)
            block(REM, 2)
            forward(REM, 3)
            forward(REM, 2)

    mine = (d // 4 + x) % 2
    for kind in (OWN, REM):
        @pl.when(mine == kind)
        def _():
            for i, (slot, slots, group, groups) in enumerate(PIECES[kind]):
                for o in range(1, 4):
                    other = (z + o) % 4
                    landed = parts.at[other, pl.ds(slot, slots), pl.ds(group, groups)]
                    pltpu.make_async_copy(landed, landed, r_recv.at[i, other]).wait()

    total = chip[mine, z % 2]
    for o in range(1, 4):
        total = total + parts[(z + o) % 4]
    red[...] = total

    def plane_copy(o):
        peer = (p + o) % 4
        return pltpu.make_async_remote_copy(
            src_ref=red.at[:, peer], dst_ref=plane.at[pl.ds(4 * p, 4)],
            send_sem=p_send.at[o], recv_sem=p_recv.at[p],
            device_id={"phase": peer, "slab": d}, device_id_type=MESH,
        )

    for o in range(1, 4):
        plane_copy(o).start()
    plane[pl.ds(4 * p, 4)] = red[:, p]
    for o in range(1, 4):
        other = (p + o) % 4
        landed = plane.at[pl.ds(4 * other, 4)]
        pltpu.make_async_copy(landed, landed, p_recv.at[other]).wait()

    def panel(half, peer):
        q = order_ref[peer]
        off = q // 4 - half
        return plane[(half * 2 + q // 2 % 2) * 4 + off * off * 2 + q % 2]

    def slab_copy(o):
        peer = (d + o) % SLABS
        return pltpu.make_async_remote_copy(
            src_ref=picked.at[o], dst_ref=gathered.at[d],
            send_sem=g_send.at[o], recv_sem=g_recv.at[d],
            device_id={"phase": p, "slab": peer}, device_id_type=MESH,
        )

    for o in range(1, SLABS):
        for half in range(2):
            picked[o, half] = panel(half, (d + o) % SLABS)
        slab_copy(o).start()
    for half in range(2):
        gathered[d, half] = panel(half, d)
    for o in range(1, SLABS):
        other = (d + o) % SLABS
        landed = gathered.at[other]
        pltpu.make_async_copy(landed, landed, g_recv.at[other]).wait()

    blades = 16
    scale = 1.0 / math.sqrt(blades)
    cosine = [round(math.cos(2 * math.pi * i / blades), 15) * scale for i in range(blades)]
    sine = [round(math.sin(2 * math.pi * i / blades), 15) * scale for i in range(blades)]
    for b in range(blades):
        real, imag = None, None
        for k in range(blades):
            c, s = cosine[k * b % blades], sine[k * b % blades]
            re, im = gathered[k % 8, k // 8, 0], gathered[k % 8, k // 8, 1]
            terms = [(re * c, im * c)] if c else []
            if s:
                terms.append((im * -s, re * s))
            for first, second in terms:
                real = first if real is None else real + first
                imag = second if imag is None else imag + second
        out_ref[0, b] = real
        out_ref[1, b] = imag

    for kind in (OWN, REM):
        for i in range(len(PIECES[kind])):
            for h in range(2):
                peer_copy(kind, i, h, lambda copy: copy.wait_send())
    for o in range(1, 4):
        plane_copy(o).wait_send()
    for o in range(1, SLABS):
        slab_copy(o).wait_send()


def fused(pressure, mode_shapes, point_weight, panel_order):
    points = pressure.shape[3]
    vmem = pltpu.VMEM
    dma = pltpu.SemaphoreType.DMA
    return pl.pallas_call(
        kernel,
        out_shape=jax.ShapeDtypeStruct((2, 16, 8, 128), F32),
        in_specs=[
            pl.BlockSpec(memory_space=pltpu.SMEM),
            pl.BlockSpec(memory_space=pl.ANY),
            pl.BlockSpec(memory_space=pl.ANY),
            pl.BlockSpec(memory_space=pltpu.VMEM),
        ],
        out_specs=pl.BlockSpec(memory_space=pltpu.VMEM),
        scratch_shapes=[
            vmem((CHUNKS, 4, 8, points), F32),
            vmem((256, points), F32),
            vmem((CHUNKS, 4, 8, points), F32),
            vmem((256, points), F32),
            vmem((512, points), BF16),
            vmem((512, points), BF16),
            vmem((512, points), BF16),
            vmem((512, points), BF16),
            vmem((2, 2, 2, 4, 4, 2, 8, 128), F32),
            vmem((2, 2, 4, 4, 2, 8, 128), F32),
            vmem((2, 2, 4, 4, 2, 8, 128), F32),
            vmem((4, 4, 4, 2, 8, 128), F32),
            vmem((4, 4, 2, 8, 128), F32),
            vmem((16, 2, 8, 128), F32),
            vmem((8, 2, 2, 8, 128), F32),
            vmem((8, 2, 2, 8, 128), F32),
            dma((CHUNKS + 1,)),
            dma((CHUNKS,)), dma((CHUNKS,)), dma((CHUNKS,)), dma((CHUNKS,)),
            dma((2, 4)), dma((2, 4)),
            dma((2, 4, 2)), dma((4, 4)),
            dma((4,)), dma((4,)),
            dma((8,)), dma((8,)),
        ],
        compiler_params=pltpu.CompilerParams(
            collective_id=0, has_side_effects=True, vmem_limit_bytes=56 * 1024 * 1024
        ),
        cost_estimate=pl.CostEstimate(
            flops=6 * 512 * 512 * points, bytes_accessed=16 * 256 * points, transcendentals=0
        ),
    )(panel_order, pressure, mode_shapes, point_weight.reshape(1, points))


def solution(mesh):
    def shards(pressure, mode_shapes, point_weight, panel_order):
        fits = (
            mesh.shape["phase"] == 4
            and mesh.shape["slab"] == SLABS
            and pressure.shape[:3] == (2, 4, 32)
            and pressure.shape[3] % 256 == 0
            and pressure.shape[3] <= 3072
            and mode_shapes.shape[0] == 256
            and panel_order.shape[0] == 8
        )
        body = fused if fits else general
        return body(pressure, mode_shapes, point_weight, panel_order)

    placed = (P(None, "phase", None, "slab"), P("phase", "slab"), P("slab"), P())
    return jax.shard_map(
        shards,
        mesh=mesh,
        in_specs=placed,
        out_specs=P(None, None, "phase", "slab"),
        check_vma=False,
    )
```

```python
import math

import jax
import jax.numpy as jnp
from jax import lax
from jax.experimental import pallas as pl
from jax.experimental.pallas import tpu as pltpu
from jax.sharding import PartitionSpec as P

MESH = pl.DeviceIdType.MESH
F32 = jnp.float32
BF16 = jnp.bfloat16
SLABS = 8
CHUNKS = 8
DEPTH = 8
OWN, REM = 0, 1


def blade_table(blades, count):
    phases = jnp.arange(count, dtype=jnp.int32)
    target = jnp.arange(blades, dtype=jnp.int32)
    index = target[:, None] * phases[None, :] % blades
    theta = index.astype(jnp.float32) * (2.0 * math.pi / blades)
    cosine = jnp.cos(theta)
    sine = jnp.sin(theta)
    upper = jnp.concatenate([cosine, -sine], axis=1)
    lower = jnp.concatenate([sine, cosine], axis=1)
    return jnp.concatenate([upper, lower], axis=0) * (1.0 / math.sqrt(blades))


def general(pressure, mode_shapes, point_weight, panel_order):
    weighted = mode_shapes * point_weight[None, :]
    phase_dev = pressure.shape[1]
    excite = pressure.shape[2]
    rows = pressure.reshape(2 * phase_dev * excite, pressure.shape[3])
    partial_forces = lax.dot_general(
        rows,
        lax.all_gather(weighted, "phase", axis=0, tiled=True),
        (((1,), (1,)), ((), ())),
        precision=lax.Precision.HIGHEST,
        preferred_element_type=jnp.float32,
    )
    row_count = partial_forces.shape[0]
    panel_count = panel_order.shape[0]
    panels = partial_forces.reshape(row_count, panel_count, -1)
    selector = (panel_order[:, None] == jnp.arange(panel_count, dtype=jnp.int32)[None, :]).astype(
        jnp.float32
    )
    reordered = jnp.einsum(
        "rqc,pq->rpc", panels, selector, precision=lax.Precision.HIGHEST
    ).reshape(row_count, -1)
    slab_count = lax.axis_size("slab")
    total = lax.psum(reordered, "slab")
    keep_width = total.shape[1] // slab_count
    share = lax.dynamic_slice_in_dim(total, lax.axis_index("slab") * keep_width, keep_width, 1)
    mode_local = share.shape[1]
    forces = share.reshape(2, phase_dev, excite, mode_local)
    blades = phase_dev * lax.axis_size("phase")
    gathered = lax.all_to_all(forces, "phase", split_axis=2, concat_axis=1, tiled=True)
    table = blade_table(blades, blades)
    result = jnp.dot(
        table,
        gathered.reshape(2 * blades, -1),
        precision=lax.Precision.HIGHEST,
        preferred_element_type=jnp.float32,
    )
    result = result.reshape(2, blades, -1, mode_local)
    return result


def split(value):
    high = value.astype(BF16)
    return high, (value - high.astype(F32)).astype(BF16)


def product(a_high, a_low, b_high, b_low):
    def dot(a, b):
        return lax.dot_general(a, b, (((1,), (1,)), ((), ())), preferred_element_type=F32)

    return dot(a_high, b_high) + dot(a_high, b_low) + dot(a_low, b_high)


PIECES = {
    OWN: ((0, 2, 0, 4), (2, 1, 0, 4), (3, 1, 0, 4)),
    REM: ((0, 3, 0, 2), (0, 3, 2, 1), (0, 3, 3, 1), (3, 1, 0, 4)),
}


def kernel(
    order_ref, a_hbm, b_hbm, w_ref, out_ref,
    a_own, b_own, a_rem, b_rem, a_hi, a_lo, b_hi, b_lo, part, sibling, chip, parts, red, plane, picked,
    gathered,
    load_sem, a_send, a_recv, b_send, b_recv, s_send, s_recv, r_send, r_recv, p_send, p_recv, g_send,
    g_recv,
):
    p = lax.axis_index("phase")
    d = lax.axis_index("slab")
    x, y = p % 2, p // 2
    z, core = d // 2, d % 2
    x_near = y * 2 + (1 - x)
    y_near = (1 - y) * 2 + x
    core_near = z * 2 + (1 - core)

    barrier = pltpu.get_barrier_semaphore()
    for o in range(1, 4):
        pl.semaphore_signal(
            barrier, inc=1, device_id={"phase": (p + o) % 4, "slab": d}, device_id_type=MESH
        )
    for o in range(1, SLABS):
        pl.semaphore_signal(
            barrier, inc=1, device_id={"phase": p, "slab": (d + o) % SLABS}, device_id_type=MESH
        )

    def a_chunk(t):
        return a_hbm.at[t % 2, :, pl.ds(8 * (t // 2), 8), :]

    loads = [pltpu.make_async_copy(a_chunk(t), a_own.at[t], load_sem.at[t]) for t in range(CHUNKS)]
    loads.append(pltpu.make_async_copy(b_hbm, b_own, load_sem.at[CHUNKS]))
    for load in loads:
        load.start()
    pl.semaphore_wait(barrier, 3 + SLABS - 1)

    def a_copy(t):
        return pltpu.make_async_remote_copy(
            src_ref=a_chunk(t), dst_ref=a_rem.at[t],
            send_sem=a_send.at[t], recv_sem=a_recv.at[t],
            device_id={"phase": x_near, "slab": d}, device_id_type=MESH,
        )

    def b_copy(t):
        return pltpu.make_async_remote_copy(
            src_ref=b_hbm.at[pl.ds(32 * t, 32)], dst_ref=b_rem.at[pl.ds(32 * t, 32)],
            send_sem=b_send.at[t], recv_sem=b_recv.at[t],
            device_id={"phase": y_near, "slab": d}, device_id_type=MESH,
        )

    def core_copy(kind, i):
        slot, slots, group, groups = PIECES[kind][i]
        where = (slice(None), pl.ds(slot, slots), pl.ds(group, groups))
        return pltpu.make_async_remote_copy(
            src_ref=part.at[(kind, 1 - core) + where], dst_ref=sibling.at[(kind,) + where],
            send_sem=s_send.at[kind, i], recv_sem=s_recv.at[kind, i],
            device_id={"phase": p, "slab": core_near}, device_id_type=MESH,
        )

    def peer_copy(kind, i, h, act):
        slot, slots, group, groups = PIECES[kind][i]
        peer_z = ((kind + x) % 2) * 2 + h
        where = (pl.ds(slot, slots), pl.ds(group, groups))

        @pl.when(peer_z != z)
        def _():
            act(pltpu.make_async_remote_copy(
                src_ref=chip.at[(kind, h) + where], dst_ref=parts.at[(z,) + where],
                send_sem=r_send.at[kind, i, h], recv_sem=r_recv.at[i, z],
                device_id={"phase": p, "slab": peer_z * 2 + core}, device_id_type=MESH,
            ))

    def forward(kind, i):
        core_copy(kind, i).wait()
        slot, slots, group, groups = PIECES[kind][i]
        for h in range(2):
            where = (h, pl.ds(slot, slots), pl.ds(group, groups))
            chip[(kind,) + where] = part[(kind, core) + where] + sibling[(kind,) + where]
            peer_copy(kind, i, h, lambda copy: copy.start())

    def split_a(source, t, kind):
        high, low = split(source[t].reshape(32, -1))
        rows = pl.ds(kind * 256 + 32 * t, 32)
        a_hi[rows], a_lo[rows] = high, low

    def split_b(source, t, kind):
        high, low = split(source[pl.ds(32 * t, 32)] * w_ref[...])
        rows = pl.ds(kind * 256 + 32 * t, 32)
        b_hi[rows], b_lo[rows] = high, low

    def block(kind, i):
        slot, slots, group, groups = PIECES[kind][i]
        rows = pl.ds(kind * 256 + 64 * group, 64 * groups)
        cols = pl.ds(128 * slot, 128 * slots)
        value = product(a_hi[rows], a_lo[rows], b_hi[cols], b_lo[cols])
        value = value.reshape(groups, 2, 4, 8, 128 * slots)
        for kk in range(4):
            for s in range(slots):
                part[kind, kk % 2, kk // 2, slot + s, pl.ds(group, groups)] = (
                    value[:, :, kk, :, 128 * s:128 * (s + 1)]
                )
        core_copy(kind, i).start()

    for t in range(DEPTH):
        a_copy(t).start()
        b_copy(t).start()

    for load in loads:
        load.wait()
    for t in range(CHUNKS):
        split_a(a_own, t, OWN)
        split_b(b_own, t, OWN)
    block(OWN, 0)

    for t in range(CHUNKS):
        b_copy(t).wait()
        if t + DEPTH < CHUNKS:
            b_copy(t + DEPTH).start()
        split_b(b_rem, t, REM)
        if t == 7:
            block(OWN, 2)
        a_copy(t).wait()
        if t + DEPTH < CHUNKS:
            a_copy(t + DEPTH).start()
        split_a(a_rem, t, REM)
        if t == 0:
            forward(OWN, 0)
        if t == 3:
            block(REM, 0)
            block(OWN, 1)
        if t == 4:
            forward(REM, 0)
            forward(OWN, 1)
        if t == 5:
            block(REM, 1)
        if t == 6:
            forward(REM, 1)
        if t == 7:
            block(REM, 3)
            forward(OWN, 2)
            block(REM, 2)
            forward(REM, 3)
            forward(REM, 2)

    mine = (d // 4 + x) % 2
    for kind in (OWN, REM):
        @pl.when(mine == kind)
        def _():
            for i, (slot, slots, group, groups) in enumerate(PIECES[kind]):
                for o in range(1, 4):
                    other = (z + o) % 4
                    landed = parts.at[other, pl.ds(slot, slots), pl.ds(group, groups)]
                    pltpu.make_async_copy(landed, landed, r_recv.at[i, other]).wait()

    total = chip[mine, z % 2]
    for o in range(1, 4):
        total = total + parts[(z + o) % 4]
    red[...] = total

    def plane_copy(o):
        peer = (p + o) % 4
        return pltpu.make_async_remote_copy(
            src_ref=red.at[:, peer], dst_ref=plane.at[pl.ds(4 * p, 4)],
            send_sem=p_send.at[o], recv_sem=p_recv.at[p],
            device_id={"phase": peer, "slab": d}, device_id_type=MESH,
        )

    for o in range(1, 4):
        plane_copy(o).start()
    plane[pl.ds(4 * p, 4)] = red[:, p]
    for o in range(1, 4):
        other = (p + o) % 4
        landed = plane.at[pl.ds(4 * other, 4)]
        pltpu.make_async_copy(landed, landed, p_recv.at[other]).wait()

    def panel(half, peer):
        q = order_ref[peer]
        off = q // 4 - half
        return plane[(half * 2 + q // 2 % 2) * 4 + off * off * 2 + q % 2]

    def slab_copy(o):
        peer = (d + o) % SLABS
        return pltpu.make_async_remote_copy(
            src_ref=picked.at[o], dst_ref=gathered.at[d],
            send_sem=g_send.at[o], recv_sem=g_recv.at[d],
            device_id={"phase": p, "slab": peer}, device_id_type=MESH,
        )

    for o in range(1, SLABS):
        for half in range(2):
            picked[o, half] = panel(half, (d + o) % SLABS)
        slab_copy(o).start()
    for half in range(2):
        gathered[d, half] = panel(half, d)
    for o in range(1, SLABS):
        other = (d + o) % SLABS
        landed = gathered.at[other]
        pltpu.make_async_copy(landed, landed, g_recv.at[other]).wait()

    blades = 16
    scale = 1.0 / math.sqrt(blades)
    cosine = [round(math.cos(2 * math.pi * i / blades), 15) * scale for i in range(blades)]
    sine = [round(math.sin(2 * math.pi * i / blades), 15) * scale for i in range(blades)]
    for b in range(blades):
        real, imag = None, None
        for k in range(blades):
            c, s = cosine[k * b % blades], sine[k * b % blades]
            re, im = gathered[k % 8, k // 8, 0], gathered[k % 8, k // 8, 1]
            terms = [(re * c, im * c)] if c else []
            if s:
                terms.append((im * -s, re * s))
            for first, second in terms:
                real = first if real is None else real + first
                imag = second if imag is None else imag + second
        out_ref[0, b] = real
        out_ref[1, b] = imag

    for kind in (OWN, REM):
        for i in range(len(PIECES[kind])):
            for h in range(2):
                peer_copy(kind, i, h, lambda copy: copy.wait_send())
    for o in range(1, 4):
        plane_copy(o).wait_send()
    for o in range(1, SLABS):
        slab_copy(o).wait_send()


def fused(pressure, mode_shapes, point_weight, panel_order):
    points = pressure.shape[3]
    vmem = pltpu.VMEM
    dma = pltpu.SemaphoreType.DMA
    return pl.pallas_call(
        kernel,
        out_shape=jax.ShapeDtypeStruct((2, 16, 8, 128), F32),
        in_specs=[
            pl.BlockSpec(memory_space=pltpu.SMEM),
            pl.BlockSpec(memory_space=pl.ANY),
            pl.BlockSpec(memory_space=pl.ANY),
            pl.BlockSpec(memory_space=pltpu.VMEM),
        ],
        out_specs=pl.BlockSpec(memory_space=pltpu.VMEM),
        scratch_shapes=[
            vmem((CHUNKS, 4, 8, points), F32),
            vmem((256, points), F32),
            vmem((CHUNKS, 4, 8, points), F32),
            vmem((256, points), F32),
            vmem((512, points), BF16),
            vmem((512, points), BF16),
            vmem((512, points), BF16),
            vmem((512, points), BF16),
            vmem((2, 2, 2, 4, 4, 2, 8, 128), F32),
            vmem((2, 2, 4, 4, 2, 8, 128), F32),
            vmem((2, 2, 4, 4, 2, 8, 128), F32),
            vmem((4, 4, 4, 2, 8, 128), F32),
            vmem((4, 4, 2, 8, 128), F32),
            vmem((16, 2, 8, 128), F32),
            vmem((8, 2, 2, 8, 128), F32),
            vmem((8, 2, 2, 8, 128), F32),
            dma((CHUNKS + 1,)),
            dma((CHUNKS,)), dma((CHUNKS,)), dma((CHUNKS,)), dma((CHUNKS,)),
            dma((2, 4)), dma((2, 4)),
            dma((2, 4, 2)), dma((4, 4)),
            dma((4,)), dma((4,)),
            dma((8,)), dma((8,)),
        ],
        compiler_params=pltpu.CompilerParams(
            collective_id=0, has_side_effects=True, vmem_limit_bytes=56 * 1024 * 1024
        ),
        cost_estimate=pl.CostEstimate(
            flops=6 * 512 * 512 * points, bytes_accessed=16 * 256 * points, transcendentals=0
        ),
    )(panel_order, pressure, mode_shapes, point_weight.reshape(1, points))


def solution(mesh):
    def shards(pressure, mode_shapes, point_weight, panel_order):
        fits = (
            mesh.shape["phase"] == 4
            and mesh.shape["slab"] == SLABS
            and pressure.shape[:3] == (2, 4, 32)
            and pressure.shape[3] % 256 == 0
            and pressure.shape[3] <= 3072
            and mode_shapes.shape[0] == 256
            and panel_order.shape[0] == 8
        )
        body = fused if fits else general
        return body(pressure, mode_shapes, point_weight, panel_order)

    placed = (P(None, "phase", None, "slab"), P("phase", "slab"), P("slab"), P())
    return jax.shard_map(
        shards,
        mesh=mesh,
        in_specs=placed,
        out_specs=P(None, None, "phase", "slab"),
        check_vma=False,
    )
```

```python
import math

import jax
import jax.numpy as jnp
from jax import lax
from jax.experimental import pallas as pl
from jax.experimental.pallas import tpu as pltpu
from jax.sharding import PartitionSpec as P

MESH = pl.DeviceIdType.MESH
F32 = jnp.float32
BF16 = jnp.bfloat16
SLABS = 8
CHUNKS = 8
TWELFTHS = 12
A_SENT = tuple((t, 0, 12) for t in range(7)) + ((7, 0, 6), (7, 6, 3), (7, 9, 2), (7, 11, 1))
B_SENT = tuple((32 * t, 32, 0, 12) for t in range(4)) + (
    (128, 128, 0, 3), (128, 128, 3, 3), (128, 128, 6, 3), (128, 128, 9, 2), (128, 128, 11, 1)
)
OWN, REM = 0, 1


def blade_table(blades, count):
    phases = jnp.arange(count, dtype=jnp.int32)
    target = jnp.arange(blades, dtype=jnp.int32)
    index = target[:, None] * phases[None, :] % blades
    theta = index.astype(jnp.float32) * (2.0 * math.pi / blades)
    cosine = jnp.cos(theta)
    sine = jnp.sin(theta)
    upper = jnp.concatenate([cosine, -sine], axis=1)
    lower = jnp.concatenate([sine, cosine], axis=1)
    return jnp.concatenate([upper, lower], axis=0) * (1.0 / math.sqrt(blades))


def general(pressure, mode_shapes, point_weight, panel_order):
    weighted = mode_shapes * point_weight[None, :]
    phase_dev = pressure.shape[1]
    excite = pressure.shape[2]
    rows = pressure.reshape(2 * phase_dev * excite, pressure.shape[3])
    partial_forces = lax.dot_general(
        rows,
        lax.all_gather(weighted, "phase", axis=0, tiled=True),
        (((1,), (1,)), ((), ())),
        precision=lax.Precision.HIGHEST,
        preferred_element_type=jnp.float32,
    )
    row_count = partial_forces.shape[0]
    panel_count = panel_order.shape[0]
    panels = partial_forces.reshape(row_count, panel_count, -1)
    selector = (panel_order[:, None] == jnp.arange(panel_count, dtype=jnp.int32)[None, :]).astype(
        jnp.float32
    )
    reordered = jnp.einsum(
        "rqc,pq->rpc", panels, selector, precision=lax.Precision.HIGHEST
    ).reshape(row_count, -1)
    slab_count = lax.axis_size("slab")
    total = lax.psum(reordered, "slab")
    keep_width = total.shape[1] // slab_count
    share = lax.dynamic_slice_in_dim(total, lax.axis_index("slab") * keep_width, keep_width, 1)
    mode_local = share.shape[1]
    forces = share.reshape(2, phase_dev, excite, mode_local)
    blades = phase_dev * lax.axis_size("phase")
    gathered = lax.all_to_all(forces, "phase", split_axis=2, concat_axis=1, tiled=True)
    table = blade_table(blades, blades)
    result = jnp.dot(
        table,
        gathered.reshape(2 * blades, -1),
        precision=lax.Precision.HIGHEST,
        preferred_element_type=jnp.float32,
    )
    result = result.reshape(2, blades, -1, mode_local)
    return result


def split(value):
    high = value.astype(BF16)
    return high, (value - high.astype(F32)).astype(BF16)


def product(a_high, a_low, b_high, b_low):
    def dot(a, b):
        return lax.dot_general(a, b, (((1,), (1,)), ((), ())), preferred_element_type=F32)

    return dot(a_high, b_high) + dot(a_high, b_low) + dot(a_low, b_high)


PIECES = {
    OWN: ((0, 2, 0, 8), (2, 1, 0, 8), (3, 1, 0, 8)),
    REM: ((0, 3, 0, 4), (0, 3, 4, 2), (0, 3, 6, 1), (0, 3, 7, 1), (3, 1, 0, 8)),
}


def kernel(
    order_ref, a_hbm, b_hbm, w_ref, out_ref,
    a_own, b_own, a_rem, b_rem, a_hi, a_lo, b_hi, b_lo, part, sibling, chip, parts, red, plane, picked,
    gathered, last_panel, last_rows,
    load_sem, a_send, a_recv, b_send, b_recv, s_send, s_recv, r_send, r_recv, p_send, p_recv, g_send,
    g_recv,
):
    p = lax.axis_index("phase")
    d = lax.axis_index("slab")
    x, y = p % 2, p // 2
    z, core = d // 2, d % 2
    x_near = y * 2 + (1 - x)
    y_near = (1 - y) * 2 + x
    core_near = z * 2 + (1 - core)

    barrier = pltpu.get_barrier_semaphore()
    for o in range(1, 4):
        pl.semaphore_signal(
            barrier, inc=1, device_id={"phase": (p + o) % 4, "slab": d}, device_id_type=MESH
        )
    for o in range(1, SLABS):
        pl.semaphore_signal(
            barrier, inc=1, device_id={"phase": p, "slab": (d + o) % SLABS}, device_id_type=MESH
        )

    def a_chunk(t):
        return a_hbm.at[t % 2, :, pl.ds(8 * (t // 2), 8), :]

    loads = [pltpu.make_async_copy(a_chunk(t), a_own.at[t], load_sem.at[t]) for t in range(CHUNKS)]
    loads.append(pltpu.make_async_copy(b_hbm, b_own, load_sem.at[CHUNKS]))
    for load in loads:
        load.start()
    pl.semaphore_wait(barrier, 3 + SLABS - 1)

    unit = a_hbm.shape[3] // TWELFTHS

    def span(first, count):
        return pl.ds(first * unit, count * unit)

    def a_copy(i):
        t, first, count = A_SENT[i]
        return pltpu.make_async_remote_copy(
            src_ref=a_chunk(t).at[:, :, span(first, count)],
            dst_ref=a_rem.at[t, :, :, span(first, count)],
            send_sem=a_send.at[i], recv_sem=a_recv.at[i],
            device_id={"phase": x_near, "slab": d}, device_id_type=MESH,
        )

    def b_copy(i):
        row, rows, first, count = B_SENT[i]
        return pltpu.make_async_remote_copy(
            src_ref=b_hbm.at[pl.ds(row, rows), span(first, count)],
            dst_ref=b_rem.at[pl.ds(row, rows), span(first, count)],
            send_sem=b_send.at[i], recv_sem=b_recv.at[i],
            device_id={"phase": y_near, "slab": d}, device_id_type=MESH,
        )

    def core_copy(kind, i):
        slot, slots, chunk, chunks = PIECES[kind][i]
        where = (slice(None), pl.ds(slot, slots), pl.ds(chunk, chunks))
        return pltpu.make_async_remote_copy(
            src_ref=part.at[(kind, 1 - core) + where], dst_ref=sibling.at[(kind,) + where],
            send_sem=s_send.at[kind, i], recv_sem=s_recv.at[kind, i],
            device_id={"phase": p, "slab": core_near}, device_id_type=MESH,
        )

    def peer_copy(kind, i, h, act):
        slot, slots, chunk, chunks = PIECES[kind][i]
        peer_z = ((kind + x) % 2) * 2 + h
        where = (pl.ds(slot, slots), pl.ds(chunk, chunks))

        @pl.when(peer_z != z)
        def _():
            act(pltpu.make_async_remote_copy(
                src_ref=chip.at[(kind, h) + where], dst_ref=parts.at[(z,) + where],
                send_sem=r_send.at[kind, i, h], recv_sem=r_recv.at[i, z],
                device_id={"phase": p, "slab": peer_z * 2 + core}, device_id_type=MESH,
            ))

    def forward(kind, i):
        core_copy(kind, i).wait()
        slot, slots, chunk, chunks = PIECES[kind][i]
        for h in range(2):
            where = (h, pl.ds(slot, slots), pl.ds(chunk, chunks))
            chip[(kind,) + where] = part[(kind, core) + where] + sibling[(kind,) + where]
            peer_copy(kind, i, h, lambda copy: copy.start())

    def split_a(source, kind, t, first, count):
        high, low = split(source[t, :, :, span(first, count)].reshape(32, count * unit))
        rows = pl.ds(kind * 256 + 32 * t, 32)
        a_hi[rows, span(first, count)], a_lo[rows, span(first, count)] = high, low

    def split_b(source, kind, row, count_rows, first, count):
        cut = span(first, count)
        for r in range(row, row + count_rows, 32):
            high, low = split(source[pl.ds(r, 32), cut] * w_ref[:, cut])
            rows = pl.ds(kind * 256 + r, 32)
            b_hi[rows, cut], b_lo[rows, cut] = high, low

    def forces(row, rows, col, cols, first=0, count=TWELFTHS):
        a_at, b_at, cut = pl.ds(row, rows), pl.ds(col, cols), span(first, count)
        return product(a_hi[a_at, cut], a_lo[a_at, cut], b_hi[b_at, cut], b_lo[b_at, cut])

    def put(kind, i, value):
        slot, slots, chunk, chunks = PIECES[kind][i]
        value = value.reshape(chunks, 4, 8, 128 * slots)
        for kk in range(4):
            for s in range(slots):
                part[kind, kk % 2, kk // 2, slot + s, pl.ds(chunk, chunks)] = (
                    value[:, kk, :, 128 * s:128 * (s + 1)]
                )
        core_copy(kind, i).start()

    def block(kind, i):
        slot, slots, chunk, chunks = PIECES[kind][i]
        put(kind, i, forces(kind * 256 + 32 * chunk, 32 * chunks, 128 * slot, 128 * slots))

    def take_a(i):
        a_copy(i).wait()
        split_a(a_rem, REM, *A_SENT[i])

    def take_b(i):
        b_copy(i).wait()
        split_b(b_rem, REM, *B_SENT[i])

    for i in range(max(len(A_SENT), len(B_SENT))):
        if i < len(A_SENT):
            a_copy(i).start()
        if i < len(B_SENT):
            b_copy(i).start()

    for load in loads:
        load.wait()
    for t in range(CHUNKS):
        split_a(a_own, OWN, t, 0, TWELFTHS)
        split_b(b_own, OWN, 32 * t, 32, 0, TWELFTHS)
    block(OWN, 0)

    for i in range(4):
        take_a(i)
        take_b(i)
        if i == 0:
            forward(OWN, 0)
    block(REM, 0)
    block(OWN, 1)
    take_a(4)
    take_b(4)
    forward(REM, 0)
    forward(OWN, 1)
    take_a(5)
    take_b(5)
    block(REM, 1)
    take_a(6)
    take_b(6)
    forward(REM, 1)
    block(REM, 2)
    last_panel[pl.ds(0, 480)] = forces(0, 480, 384, 128, 0, 9)
    take_a(7)
    forward(REM, 2)
    value = forces(480, 32, 0, 512, 0, 6)
    last_rows[...] = value[:, :384]
    last_panel[pl.ds(480, 32)] = value[:, 384:]
    take_b(7)
    last_panel[pl.ds(0, 480)] += forces(0, 480, 384, 128, 9, 2)
    take_a(8)
    value = forces(480, 32, 0, 512, 6, 3)
    last_rows[...] += value[:, :384]
    last_panel[pl.ds(480, 32)] += value[:, 384:]
    take_a(9)
    value = forces(480, 32, 0, 512, 9, 2)
    last_rows[...] += value[:, :384]
    last_panel[pl.ds(480, 32)] += value[:, 384:]
    take_b(8)
    put(OWN, 2, last_panel[pl.ds(0, 256)] + forces(0, 256, 384, 128, 11, 1))
    take_a(10)
    put(REM, 4, last_panel[pl.ds(256, 256)] + forces(256, 256, 384, 128, 11, 1))
    put(REM, 3, last_rows[...] + forces(480, 32, 0, 384, 11, 1))
    forward(OWN, 2)
    forward(REM, 4)
    forward(REM, 3)

    mine = (d // 4 + x) % 2
    for kind in (OWN, REM):
        @pl.when(mine == kind)
        def _():
            for i, (slot, slots, chunk, chunks) in enumerate(PIECES[kind]):
                for o in range(1, 4):
                    other = (z + o) % 4
                    landed = parts.at[other, pl.ds(slot, slots), pl.ds(chunk, chunks)]
                    pltpu.make_async_copy(landed, landed, r_recv.at[i, other]).wait()

    total = chip[mine, z % 2]
    for o in range(1, 4):
        total = total + parts[(z + o) % 4]
    red[...] = total

    def plane_copy(o):
        peer = (p + o) % 4
        return pltpu.make_async_remote_copy(
            src_ref=red.at[:, pl.ds(2 * peer, 2)], dst_ref=plane.at[pl.ds(4 * p, 4)],
            send_sem=p_send.at[o], recv_sem=p_recv.at[p],
            device_id={"phase": peer, "slab": d}, device_id_type=MESH,
        )

    for o in range(1, 4):
        plane_copy(o).start()
    plane[pl.ds(4 * p, 4)] = red[:, pl.ds(2 * p, 2)]
    for o in range(1, 4):
        other = (p + o) % 4
        landed = plane.at[pl.ds(4 * other, 4)]
        pltpu.make_async_copy(landed, landed, p_recv.at[other]).wait()

    def panel(half, peer):
        q = order_ref[peer]
        off = q // 4 - half
        return plane[(half * 2 + q // 2 % 2) * 4 + off * off * 2 + q % 2]

    def slab_copy(o):
        peer = (d + o) % SLABS
        return pltpu.make_async_remote_copy(
            src_ref=picked.at[o], dst_ref=gathered.at[d],
            send_sem=g_send.at[o], recv_sem=g_recv.at[d],
            device_id={"phase": p, "slab": peer}, device_id_type=MESH,
        )

    for o in range(1, SLABS):
        for half in range(2):
            picked[o, half] = panel(half, (d + o) % SLABS)
        slab_copy(o).start()
    for half in range(2):
        gathered[d, half] = panel(half, d)
    for o in range(1, SLABS):
        other = (d + o) % SLABS
        landed = gathered.at[other]
        pltpu.make_async_copy(landed, landed, g_recv.at[other]).wait()

    blades = 16
    scale = 1.0 / math.sqrt(blades)
    cosine = [round(math.cos(2 * math.pi * i / blades), 15) * scale for i in range(blades)]
    sine = [round(math.sin(2 * math.pi * i / blades), 15) * scale for i in range(blades)]
    for b in range(blades):
        real, imag = None, None
        for k in range(blades):
            c, s = cosine[k * b % blades], sine[k * b % blades]
            re, im = gathered[k % 8, k // 8, 0], gathered[k % 8, k // 8, 1]
            terms = [(re * c, im * c)] if c else []
            if s:
                terms.append((im * -s, re * s))
            for first, second in terms:
                real = first if real is None else real + first
                imag = second if imag is None else imag + second
        out_ref[0, b] = real
        out_ref[1, b] = imag

    for kind in (OWN, REM):
        for i in range(len(PIECES[kind])):
            for h in range(2):
                peer_copy(kind, i, h, lambda copy: copy.wait_send())
    for o in range(1, 4):
        plane_copy(o).wait_send()
    for o in range(1, SLABS):
        slab_copy(o).wait_send()


def fused(pressure, mode_shapes, point_weight, panel_order):
    points = pressure.shape[3]
    vmem = pltpu.VMEM
    dma = pltpu.SemaphoreType.DMA
    return pl.pallas_call(
        kernel,
        out_shape=jax.ShapeDtypeStruct((2, 16, 8, 128), F32),
        in_specs=[
            pl.BlockSpec(memory_space=pltpu.SMEM),
            pl.BlockSpec(memory_space=pl.ANY),
            pl.BlockSpec(memory_space=pl.ANY),
            pl.BlockSpec(memory_space=pltpu.VMEM),
        ],
        out_specs=pl.BlockSpec(memory_space=pltpu.VMEM),
        scratch_shapes=[
            vmem((CHUNKS, 4, 8, points), F32),
            vmem((256, points), F32),
            vmem((CHUNKS, 4, 8, points), F32),
            vmem((256, points), F32),
            vmem((512, points), BF16),
            vmem((512, points), BF16),
            vmem((512, points), BF16),
            vmem((512, points), BF16),
            vmem((2, 2, 2, 4, CHUNKS, 8, 128), F32),
            vmem((2, 2, 4, CHUNKS, 8, 128), F32),
            vmem((2, 2, 4, CHUNKS, 8, 128), F32),
            vmem((4, 4, CHUNKS, 8, 128), F32),
            vmem((4, CHUNKS, 8, 128), F32),
            vmem((16, 2, 8, 128), F32),
            vmem((8, 2, 2, 8, 128), F32),
            vmem((8, 2, 2, 8, 128), F32),
            vmem((512, 128), F32),
            vmem((32, 384), F32),
            dma((CHUNKS + 1,)),
            dma((len(A_SENT),)), dma((len(A_SENT),)), dma((len(B_SENT),)), dma((len(B_SENT),)),
            dma((2, 5)), dma((2, 5)),
            dma((2, 5, 2)), dma((5, 4)),
            dma((4,)), dma((4,)),
            dma((8,)), dma((8,)),
        ],
        compiler_params=pltpu.CompilerParams(
            collective_id=0, has_side_effects=True, vmem_limit_bytes=56 * 1024 * 1024
        ),
        cost_estimate=pl.CostEstimate(
            flops=6 * 512 * 512 * points, bytes_accessed=16 * 256 * points, transcendentals=0
        ),
    )(panel_order, pressure, mode_shapes, point_weight.reshape(1, points))


def solution(mesh):
    def shards(pressure, mode_shapes, point_weight, panel_order):
        fits = (
            mesh.shape["phase"] == 4
            and mesh.shape["slab"] == SLABS
            and pressure.shape[:3] == (2, 4, 32)
            and pressure.shape[3] % 1536 == 0
            and pressure.shape[3] <= 3072
            and mode_shapes.shape[0] == 256
            and panel_order.shape[0] == 8
        )
        body = fused if fits else general
        return body(pressure, mode_shapes, point_weight, panel_order)

    placed = (P(None, "phase", None, "slab"), P("phase", "slab"), P("slab"), P())
    return jax.shard_map(
        shards,
        mesh=mesh,
        in_specs=placed,
        out_specs=P(None, None, "phase", "slab"),
        check_vma=False,
    )
```

```python
import math

import jax
import jax.numpy as jnp
from jax import lax
from jax.experimental import pallas as pl
from jax.experimental.pallas import tpu as pltpu
from jax.sharding import PartitionSpec as P

MESH = pl.DeviceIdType.MESH
F32 = jnp.float32
BF16 = jnp.bfloat16
SLABS = 8
CHUNKS = 8
TWELFTHS = 12
A_SENT = tuple((t, 0, 12) for t in range(7)) + ((7, 0, 6), (7, 6, 3), (7, 9, 2), (7, 11, 1))
B_SENT = tuple((32 * t, 32, 0, 12) for t in range(7)) + (
    (224, 32, 0, 6), (224, 32, 6, 3), (224, 32, 9, 2), (224, 32, 11, 1)
)
OWN, REM = 0, 1


def blade_table(blades, count):
    phases = jnp.arange(count, dtype=jnp.int32)
    target = jnp.arange(blades, dtype=jnp.int32)
    index = target[:, None] * phases[None, :] % blades
    theta = index.astype(jnp.float32) * (2.0 * math.pi / blades)
    cosine = jnp.cos(theta)
    sine = jnp.sin(theta)
    upper = jnp.concatenate([cosine, -sine], axis=1)
    lower = jnp.concatenate([sine, cosine], axis=1)
    return jnp.concatenate([upper, lower], axis=0) * (1.0 / math.sqrt(blades))


def general(pressure, mode_shapes, point_weight, panel_order):
    weighted = mode_shapes * point_weight[None, :]
    phase_dev = pressure.shape[1]
    excite = pressure.shape[2]
    rows = pressure.reshape(2 * phase_dev * excite, pressure.shape[3])
    partial_forces = lax.dot_general(
        rows,
        lax.all_gather(weighted, "phase", axis=0, tiled=True),
        (((1,), (1,)), ((), ())),
        precision=lax.Precision.HIGHEST,
        preferred_element_type=jnp.float32,
    )
    row_count = partial_forces.shape[0]
    panel_count = panel_order.shape[0]
    panels = partial_forces.reshape(row_count, panel_count, -1)
    selector = (panel_order[:, None] == jnp.arange(panel_count, dtype=jnp.int32)[None, :]).astype(
        jnp.float32
    )
    reordered = jnp.einsum(
        "rqc,pq->rpc", panels, selector, precision=lax.Precision.HIGHEST
    ).reshape(row_count, -1)
    slab_count = lax.axis_size("slab")
    total = lax.psum(reordered, "slab")
    keep_width = total.shape[1] // slab_count
    share = lax.dynamic_slice_in_dim(total, lax.axis_index("slab") * keep_width, keep_width, 1)
    mode_local = share.shape[1]
    forces = share.reshape(2, phase_dev, excite, mode_local)
    blades = phase_dev * lax.axis_size("phase")
    gathered = lax.all_to_all(forces, "phase", split_axis=2, concat_axis=1, tiled=True)
    table = blade_table(blades, blades)
    result = jnp.dot(
        table,
        gathered.reshape(2 * blades, -1),
        precision=lax.Precision.HIGHEST,
        preferred_element_type=jnp.float32,
    )
    result = result.reshape(2, blades, -1, mode_local)
    return result


def split(value):
    high = value.astype(BF16)
    return high, (value - high.astype(F32)).astype(BF16)


def product(a_high, a_low, b_high, b_low):
    def dot(a, b):
        return lax.dot_general(a, b, (((1,), (1,)), ((), ())), preferred_element_type=F32)

    return dot(a_high, b_high) + dot(a_high, b_low) + dot(a_low, b_high)


PIECES = {
    OWN: ((0, 2, 0, 8), (2, 1, 0, 8), (3, 1, 0, 8), (4, 1, 0, 2)),
    REM: ((0, 3, 0, 4), (0, 3, 4, 2), (0, 3, 6, 1), (3, 1, 0, 7), (4, 1, 0, 2), (0, 4, 7, 1)),
}


def kernel(
    order_ref, a_hbm, b_hbm, w_ref, out_ref,
    a_own, b_own, a_rem, b_rem, a_hi, a_lo, b_hi, b_lo, part, sibling, chip, parts, red, plane, picked,
    gathered, last_cols, last_rows,
    load_sem, a_send, a_recv, b_send, b_recv, s_send, s_recv, r_send, r_recv, p_send, p_recv, g_send,
    g_recv,
):
    p = lax.axis_index("phase")
    d = lax.axis_index("slab")
    x, y = p % 2, p // 2
    z, core = d // 2, d % 2
    x_near = y * 2 + (1 - x)
    y_near = (1 - y) * 2 + x
    core_near = z * 2 + (1 - core)

    barrier = pltpu.get_barrier_semaphore()
    for o in range(1, 4):
        pl.semaphore_signal(
            barrier, inc=1, device_id={"phase": (p + o) % 4, "slab": d}, device_id_type=MESH
        )
    for o in range(1, SLABS):
        pl.semaphore_signal(
            barrier, inc=1, device_id={"phase": p, "slab": (d + o) % SLABS}, device_id_type=MESH
        )

    def a_chunk(t):
        return a_hbm.at[t % 2, :, pl.ds(8 * (t // 2), 8), :]

    loads = [pltpu.make_async_copy(a_chunk(t), a_own.at[t], load_sem.at[t]) for t in range(CHUNKS)]
    loads.append(pltpu.make_async_copy(b_hbm, b_own, load_sem.at[CHUNKS]))
    for load in loads:
        load.start()
    pl.semaphore_wait(barrier, 3 + SLABS - 1)

    unit = a_hbm.shape[3] // TWELFTHS

    def span(first, count):
        return pl.ds(first * unit, count * unit)

    def a_copy(i):
        t, first, count = A_SENT[i]
        return pltpu.make_async_remote_copy(
            src_ref=a_chunk(t).at[:, :, span(first, count)],
            dst_ref=a_rem.at[t, :, :, span(first, count)],
            send_sem=a_send.at[i], recv_sem=a_recv.at[i],
            device_id={"phase": x_near, "slab": d}, device_id_type=MESH,
        )

    def b_copy(i):
        row, rows, first, count = B_SENT[i]
        return pltpu.make_async_remote_copy(
            src_ref=b_hbm.at[pl.ds(row, rows), span(first, count)],
            dst_ref=b_rem.at[pl.ds(row, rows), span(first, count)],
            send_sem=b_send.at[i], recv_sem=b_recv.at[i],
            device_id={"phase": y_near, "slab": d}, device_id_type=MESH,
        )

    def core_copy(kind, i):
        slot, slots, chunk, chunks = PIECES[kind][i]
        where = (slice(None), pl.ds(slot, slots), pl.ds(chunk, chunks))
        return pltpu.make_async_remote_copy(
            src_ref=part.at[(kind, 1 - core) + where], dst_ref=sibling.at[(kind,) + where],
            send_sem=s_send.at[kind, i], recv_sem=s_recv.at[kind, i],
            device_id={"phase": p, "slab": core_near}, device_id_type=MESH,
        )

    def peer_copy(kind, i, h, act):
        slot, slots, chunk, chunks = PIECES[kind][i]
        peer_z = ((kind + x) % 2) * 2 + h
        where = (pl.ds(slot, slots), pl.ds(chunk, chunks))

        @pl.when(peer_z != z)
        def _():
            act(pltpu.make_async_remote_copy(
                src_ref=chip.at[(kind, h) + where], dst_ref=parts.at[(z,) + where],
                send_sem=r_send.at[kind, i, h], recv_sem=r_recv.at[i, z],
                device_id={"phase": p, "slab": peer_z * 2 + core}, device_id_type=MESH,
            ))

    def forward(kind, i):
        core_copy(kind, i).wait()
        slot, slots, chunk, chunks = PIECES[kind][i]
        for h in range(2):
            where = (h, pl.ds(slot, slots), pl.ds(chunk, chunks))
            chip[(kind,) + where] = part[(kind, core) + where] + sibling[(kind,) + where]
            peer_copy(kind, i, h, lambda copy: copy.start())

    def split_a(source, kind, t, first, count):
        high, low = split(source[t, :, :, span(first, count)].reshape(32, count * unit))
        rows = pl.ds(kind * 256 + 32 * t, 32)
        a_hi[rows, span(first, count)], a_lo[rows, span(first, count)] = high, low

    def split_b(source, kind, row, count_rows, first, count):
        cut = span(first, count)
        for r in range(row, row + count_rows, 32):
            high, low = split(source[pl.ds(r, 32), cut] * w_ref[:, cut])
            rows = pl.ds(kind * 256 + r, 32)
            b_hi[rows, cut], b_lo[rows, cut] = high, low

    def forces(row, rows, col, cols, first=0, count=TWELFTHS):
        a_at, b_at, cut = pl.ds(row, rows), pl.ds(col, cols), span(first, count)
        return product(a_hi[a_at, cut], a_lo[a_at, cut], b_hi[b_at, cut], b_lo[b_at, cut])

    def put(kind, i, value):
        slot, slots, chunk, chunks = PIECES[kind][i]
        value = value.reshape(chunks, 4, 8, 128 * slots)
        for kk in range(4):
            for s in range(slots):
                part[kind, kk % 2, kk // 2, slot + s, pl.ds(chunk, chunks)] = (
                    value[:, kk, :, 128 * s:128 * (s + 1)]
                )
        core_copy(kind, i).start()

    def block(kind, i):
        slot, slots, chunk, chunks = PIECES[kind][i]
        put(kind, i, forces(kind * 256 + 32 * chunk, 32 * chunks, 128 * slot, 128 * slots))

    def take_a(i):
        a_copy(i).wait()
        split_a(a_rem, REM, *A_SENT[i])

    def take_b(i):
        b_copy(i).wait()
        split_b(b_rem, REM, *B_SENT[i])

    for i in range(max(len(A_SENT), len(B_SENT))):
        if i < len(A_SENT):
            a_copy(i).start()
        if i < len(B_SENT):
            b_copy(i).start()

    for load in loads:
        load.wait()
    for t in range(CHUNKS):
        split_a(a_own, OWN, t, 0, TWELFTHS)
        split_b(b_own, OWN, 32 * t, 32, 0, TWELFTHS)
    block(OWN, 0)

    for i in range(4):
        take_a(i)
        take_b(i)
        if i == 0:
            forward(OWN, 0)
    block(REM, 0)
    block(OWN, 1)
    take_a(4)
    take_b(4)
    forward(REM, 0)
    forward(OWN, 1)
    take_a(5)
    take_b(5)
    block(REM, 1)
    take_a(6)
    take_b(6)
    forward(REM, 1)
    block(REM, 2)
    lane = lax.broadcasted_iota(jnp.int32, (4, 8, 128), 2)
    value = forces(0, 480, 384, 128)
    value = jnp.where(lax.broadcasted_iota(jnp.int32, (480, 128), 1) < 96, value, 0.0)
    put(OWN, 2, value[:256])
    put(REM, 3, value[256:])

    def late(first, count):
        return forces(0, 480, 384, 128, first, count), forces(480, 32, 0, 512, first, count)

    take_a(7)
    take_b(7)
    last_cols[...], last_rows[...] = late(0, 6)
    forward(REM, 2)
    forward(OWN, 2)
    forward(REM, 3)
    for i, first, count in ((8, 6, 3), (9, 9, 2)):
        take_a(i)
        take_b(i)
        cols, rows = late(first, count)
        last_cols[...] += cols
        last_rows[...] += rows
    take_a(10)
    take_b(10)
    cols, rows = late(11, 1)
    put(REM, 5, last_rows[...] + rows)
    cols = last_cols[...] + cols
    for kind in (REM, OWN):
        for c in range(2):
            packed = jnp.zeros((4, 8, 128), F32)
            for g in range(4):
                at = kind * 256 + 32 * (2 * g + c)
                if at >= 480:
                    continue
                moved = cols[at:at + 32].reshape(4, 8, 128)
                if g < 3:
                    moved = pltpu.roll(moved, 32 * (g + 1), 2)
                inside = jnp.logical_and(lane >= 32 * g, lane < 32 * (g + 1))
                packed = jnp.where(inside, moved, packed)
            for kk in range(4):
                part[kind, kk % 2, kk // 2, 4, c] = packed[kk]
        core_copy(kind, 4 if kind == REM else 3).start()
    forward(REM, 5)
    forward(REM, 4)
    forward(OWN, 3)

    mine = (d // 4 + x) % 2
    for kind in (OWN, REM):
        @pl.when(mine == kind)
        def _():
            for i, (slot, slots, chunk, chunks) in enumerate(PIECES[kind]):
                for o in range(1, 4):
                    other = (z + o) % 4
                    landed = parts.at[other, pl.ds(slot, slots), pl.ds(chunk, chunks)]
                    pltpu.make_async_copy(landed, landed, r_recv.at[i, other]).wait()

    total = chip[mine, z % 2]
    for o in range(1, 4):
        total = total + parts[(z + o) % 4]
    red[...] = total[:4]
    for c in range(2):
        for g in range(4):
            moved = total[4, c]
            if g < 3:
                moved = pltpu.roll(moved, 96 - 32 * g, 1)
            red[3, 2 * g + c] = total[3, 2 * g + c] + jnp.where(lane[0] >= 96, moved, 0.0)

    def plane_copy(o):
        peer = (p + o) % 4
        return pltpu.make_async_remote_copy(
            src_ref=red.at[:, pl.ds(2 * peer, 2)], dst_ref=plane.at[pl.ds(4 * p, 4)],
            send_sem=p_send.at[o], recv_sem=p_recv.at[p],
            device_id={"phase": peer, "slab": d}, device_id_type=MESH,
        )

    for o in range(1, 4):
        plane_copy(o).start()
    plane[pl.ds(4 * p, 4)] = red[:, pl.ds(2 * p, 2)]
    for o in range(1, 4):
        other = (p + o) % 4
        landed = plane.at[pl.ds(4 * other, 4)]
        pltpu.make_async_copy(landed, landed, p_recv.at[other]).wait()

    def panel(half, peer):
        q = order_ref[peer]
        off = q // 4 - half
        return plane[(half * 2 + q // 2 % 2) * 4 + off * off * 2 + q % 2]

    def slab_copy(o):
        peer = (d + o) % SLABS
        return pltpu.make_async_remote_copy(
            src_ref=picked.at[o], dst_ref=gathered.at[d],
            send_sem=g_send.at[o], recv_sem=g_recv.at[d],
            device_id={"phase": p, "slab": peer}, device_id_type=MESH,
        )

    for o in range(1, SLABS):
        for half in range(2):
            picked[o, half] = panel(half, (d + o) % SLABS)
        slab_copy(o).start()
    for half in range(2):
        gathered[d, half] = panel(half, d)
    for o in range(1, SLABS):
        other = (d + o) % SLABS
        landed = gathered.at[other]
        pltpu.make_async_copy(landed, landed, g_recv.at[other]).wait()

    blades = 16
    scale = 1.0 / math.sqrt(blades)
    cosine = [round(math.cos(2 * math.pi * i / blades), 15) * scale for i in range(blades)]
    sine = [round(math.sin(2 * math.pi * i / blades), 15) * scale for i in range(blades)]
    for b in range(blades):
        real, imag = None, None
        for k in range(blades):
            c, s = cosine[k * b % blades], sine[k * b % blades]
            re, im = gathered[k % 8, k // 8, 0], gathered[k % 8, k // 8, 1]
            terms = [(re * c, im * c)] if c else []
            if s:
                terms.append((im * -s, re * s))
            for first, second in terms:
                real = first if real is None else real + first
                imag = second if imag is None else imag + second
        out_ref[0, b] = real
        out_ref[1, b] = imag

    for kind in (OWN, REM):
        for i in range(len(PIECES[kind])):
            for h in range(2):
                peer_copy(kind, i, h, lambda copy: copy.wait_send())
    for o in range(1, 4):
        plane_copy(o).wait_send()
    for o in range(1, SLABS):
        slab_copy(o).wait_send()


def fused(pressure, mode_shapes, point_weight, panel_order):
    points = pressure.shape[3]
    vmem = pltpu.VMEM
    dma = pltpu.SemaphoreType.DMA
    return pl.pallas_call(
        kernel,
        out_shape=jax.ShapeDtypeStruct((2, 16, 8, 128), F32),
        in_specs=[
            pl.BlockSpec(memory_space=pltpu.SMEM),
            pl.BlockSpec(memory_space=pl.ANY),
            pl.BlockSpec(memory_space=pl.ANY),
            pl.BlockSpec(memory_space=pltpu.VMEM),
        ],
        out_specs=pl.BlockSpec(memory_space=pltpu.VMEM),
        scratch_shapes=[
            vmem((CHUNKS, 4, 8, points), F32),
            vmem((256, points), F32),
            vmem((CHUNKS, 4, 8, points), F32),
            vmem((256, points), F32),
            vmem((512, points), BF16),
            vmem((512, points), BF16),
            vmem((512, points), BF16),
            vmem((512, points), BF16),
            vmem((2, 2, 2, 5, CHUNKS, 8, 128), F32),
            vmem((2, 2, 5, CHUNKS, 8, 128), F32),
            vmem((2, 2, 5, CHUNKS, 8, 128), F32),
            vmem((4, 5, CHUNKS, 8, 128), F32),
            vmem((4, CHUNKS, 8, 128), F32),
            vmem((16, 2, 8, 128), F32),
            vmem((8, 2, 2, 8, 128), F32),
            vmem((8, 2, 2, 8, 128), F32),
            vmem((480, 128), F32),
            vmem((32, 512), F32),
            dma((CHUNKS + 1,)),
            dma((len(A_SENT),)), dma((len(A_SENT),)), dma((len(B_SENT),)), dma((len(B_SENT),)),
            dma((2, 6)), dma((2, 6)),
            dma((2, 6, 2)), dma((6, 4)),
            dma((4,)), dma((4,)),
            dma((8,)), dma((8,)),
        ],
        compiler_params=pltpu.CompilerParams(
            collective_id=0, has_side_effects=True, vmem_limit_bytes=56 * 1024 * 1024
        ),
        cost_estimate=pl.CostEstimate(
            flops=6 * 512 * 512 * points, bytes_accessed=16 * 256 * points, transcendentals=0
        ),
    )(panel_order, pressure, mode_shapes, point_weight.reshape(1, points))


def solution(mesh):
    def shards(pressure, mode_shapes, point_weight, panel_order):
        fits = (
            mesh.shape["phase"] == 4
            and mesh.shape["slab"] == SLABS
            and pressure.shape[:3] == (2, 4, 32)
            and pressure.shape[3] % 1536 == 0
            and pressure.shape[3] <= 3072
            and mode_shapes.shape[0] == 256
            and panel_order.shape[0] == 8
        )
        body = fused if fits else general
        return body(pressure, mode_shapes, point_weight, panel_order)

    placed = (P(None, "phase", None, "slab"), P("phase", "slab"), P("slab"), P())
    return jax.shard_map(
        shards,
        mesh=mesh,
        in_specs=placed,
        out_specs=P(None, None, "phase", "slab"),
        check_vma=False,
    )
```

```python
import math

import jax
import jax.numpy as jnp
from jax import lax
from jax.experimental import pallas as pl
from jax.experimental.pallas import tpu as pltpu
from jax.sharding import PartitionSpec as P

MESH = pl.DeviceIdType.MESH
F32 = jnp.float32
BF16 = jnp.bfloat16
SLABS = 8
CHUNKS = 8
TWELFTHS = 12
A_SENT = tuple((t, 0, 12) for t in range(7)) + ((7, 0, 6), (7, 6, 3), (7, 9, 2), (7, 11, 1))
B_SENT = tuple((32 * t, 32, 0, 12) for t in range(4)) + (
    (128, 128, 0, 3), (128, 128, 3, 3), (128, 128, 6, 3), (128, 128, 9, 2), (128, 128, 11, 1)
)
OWN, REM = 0, 1


def blade_table(blades, count):
    phases = jnp.arange(count, dtype=jnp.int32)
    target = jnp.arange(blades, dtype=jnp.int32)
    index = target[:, None] * phases[None, :] % blades
    theta = index.astype(jnp.float32) * (2.0 * math.pi / blades)
    cosine = jnp.cos(theta)
    sine = jnp.sin(theta)
    upper = jnp.concatenate([cosine, -sine], axis=1)
    lower = jnp.concatenate([sine, cosine], axis=1)
    return jnp.concatenate([upper, lower], axis=0) * (1.0 / math.sqrt(blades))


def general(pressure, mode_shapes, point_weight, panel_order):
    weighted = mode_shapes * point_weight[None, :]
    phase_dev = pressure.shape[1]
    excite = pressure.shape[2]
    rows = pressure.reshape(2 * phase_dev * excite, pressure.shape[3])
    partial_forces = lax.dot_general(
        rows,
        lax.all_gather(weighted, "phase", axis=0, tiled=True),
        (((1,), (1,)), ((), ())),
        precision=lax.Precision.HIGHEST,
        preferred_element_type=jnp.float32,
    )
    row_count = partial_forces.shape[0]
    panel_count = panel_order.shape[0]
    panels = partial_forces.reshape(row_count, panel_count, -1)
    selector = (panel_order[:, None] == jnp.arange(panel_count, dtype=jnp.int32)[None, :]).astype(
        jnp.float32
    )
    reordered = jnp.einsum(
        "rqc,pq->rpc", panels, selector, precision=lax.Precision.HIGHEST
    ).reshape(row_count, -1)
    slab_count = lax.axis_size("slab")
    total = lax.psum(reordered, "slab")
    keep_width = total.shape[1] // slab_count
    share = lax.dynamic_slice_in_dim(total, lax.axis_index("slab") * keep_width, keep_width, 1)
    mode_local = share.shape[1]
    forces = share.reshape(2, phase_dev, excite, mode_local)
    blades = phase_dev * lax.axis_size("phase")
    gathered = lax.all_to_all(forces, "phase", split_axis=2, concat_axis=1, tiled=True)
    table = blade_table(blades, blades)
    result = jnp.dot(
        table,
        gathered.reshape(2 * blades, -1),
        precision=lax.Precision.HIGHEST,
        preferred_element_type=jnp.float32,
    )
    result = result.reshape(2, blades, -1, mode_local)
    return result


def split(value):
    high = value.astype(BF16)
    return high, (value - high.astype(F32)).astype(BF16)


def product(a_high, a_low, b_high, b_low):
    def dot(a, b):
        return lax.dot_general(a, b, (((1,), (1,)), ((), ())), preferred_element_type=F32)

    return dot(a_high, b_high) + dot(a_high, b_low) + dot(a_low, b_high)


PIECES = {
    OWN: ((0, 2, 0, 8), (2, 1, 0, 8), (3, 1, 0, 8)),
    REM: ((0, 3, 0, 4), (0, 3, 4, 2), (0, 3, 6, 1), (0, 3, 7, 1), (3, 1, 0, 8)),
}


def kernel(
    order_ref, a_hbm, b_hbm, w_ref, gathered,
    a_own, b_own, a_rem, b_rem, a_hi, a_lo, b_hi, b_lo, part, sibling, chip, parts, red, plane, picked,
    last_panel, last_rows,
    load_sem, a_send, a_recv, b_send, b_recv, s_send, s_recv, r_send, r_recv, p_send, p_recv, g_send,
    g_recv,
):
    p = lax.axis_index("phase")
    d = lax.axis_index("slab")
    x, y = p % 2, p // 2
    z, core = d // 2, d % 2
    x_near = y * 2 + (1 - x)
    y_near = (1 - y) * 2 + x
    core_near = z * 2 + (1 - core)

    barrier = pltpu.get_barrier_semaphore()
    for o in range(1, 4):
        pl.semaphore_signal(
            barrier, inc=1, device_id={"phase": (p + o) % 4, "slab": d}, device_id_type=MESH
        )
    for o in range(1, SLABS):
        pl.semaphore_signal(
            barrier, inc=1, device_id={"phase": p, "slab": (d + o) % SLABS}, device_id_type=MESH
        )

    def a_chunk(t):
        return a_hbm.at[t % 2, :, pl.ds(8 * (t // 2), 8), :]

    loads = [pltpu.make_async_copy(a_chunk(t), a_own.at[t], load_sem.at[t]) for t in range(CHUNKS)]
    loads.append(pltpu.make_async_copy(b_hbm, b_own, load_sem.at[CHUNKS]))
    for load in loads:
        load.start()
    pl.semaphore_wait(barrier, 3 + SLABS - 1)

    unit = a_hbm.shape[3] // TWELFTHS

    def span(first, count):
        return pl.ds(first * unit, count * unit)

    def a_copy(i):
        t, first, count = A_SENT[i]
        return pltpu.make_async_remote_copy(
            src_ref=a_chunk(t).at[:, :, span(first, count)],
            dst_ref=a_rem.at[t, :, :, span(first, count)],
            send_sem=a_send.at[i], recv_sem=a_recv.at[i],
            device_id={"phase": x_near, "slab": d}, device_id_type=MESH,
        )

    def b_copy(i):
        row, rows, first, count = B_SENT[i]
        return pltpu.make_async_remote_copy(
            src_ref=b_hbm.at[pl.ds(row, rows), span(first, count)],
            dst_ref=b_rem.at[pl.ds(row, rows), span(first, count)],
            send_sem=b_send.at[i], recv_sem=b_recv.at[i],
            device_id={"phase": y_near, "slab": d}, device_id_type=MESH,
        )

    def core_copy(kind, i):
        slot, slots, chunk, chunks = PIECES[kind][i]
        where = (slice(None), pl.ds(slot, slots), pl.ds(chunk, chunks))
        return pltpu.make_async_remote_copy(
            src_ref=part.at[(kind, 1 - core) + where], dst_ref=sibling.at[(kind,) + where],
            send_sem=s_send.at[kind, i], recv_sem=s_recv.at[kind, i],
            device_id={"phase": p, "slab": core_near}, device_id_type=MESH,
        )

    def peer_copy(kind, i, h, act):
        slot, slots, chunk, chunks = PIECES[kind][i]
        peer_z = ((kind + x) % 2) * 2 + h
        where = (pl.ds(slot, slots), pl.ds(chunk, chunks))

        @pl.when(peer_z != z)
        def _():
            act(pltpu.make_async_remote_copy(
                src_ref=chip.at[(kind, h) + where], dst_ref=parts.at[(z,) + where],
                send_sem=r_send.at[kind, i, h], recv_sem=r_recv.at[i, z],
                device_id={"phase": p, "slab": peer_z * 2 + core}, device_id_type=MESH,
            ))

    def forward(kind, i):
        core_copy(kind, i).wait()
        slot, slots, chunk, chunks = PIECES[kind][i]
        for h in range(2):
            where = (h, pl.ds(slot, slots), pl.ds(chunk, chunks))
            chip[(kind,) + where] = part[(kind, core) + where] + sibling[(kind,) + where]
            peer_copy(kind, i, h, lambda copy: copy.start())

    def split_a(source, kind, t, first, count):
        high, low = split(source[t, :, :, span(first, count)].reshape(32, count * unit))
        rows = pl.ds(kind * 256 + 32 * t, 32)
        a_hi[rows, span(first, count)], a_lo[rows, span(first, count)] = high, low

    def split_b(source, kind, row, count_rows, first, count):
        cut = span(first, count)
        for r in range(row, row + count_rows, 32):
            high, low = split(source[pl.ds(r, 32), cut] * w_ref[:, cut])
            rows = pl.ds(kind * 256 + r, 32)
            b_hi[rows, cut], b_lo[rows, cut] = high, low

    def forces(row, rows, col, cols, first=0, count=TWELFTHS):
        a_at, b_at, cut = pl.ds(row, rows), pl.ds(col, cols), span(first, count)
        return product(a_hi[a_at, cut], a_lo[a_at, cut], b_hi[b_at, cut], b_lo[b_at, cut])

    def put(kind, i, value):
        slot, slots, chunk, chunks = PIECES[kind][i]
        value = value.reshape(chunks, 4, 8, 128 * slots)
        for kk in range(4):
            for s in range(slots):
                part[kind, kk % 2, kk // 2, slot + s, pl.ds(chunk, chunks)] = (
                    value[:, kk, :, 128 * s:128 * (s + 1)]
                )
        core_copy(kind, i).start()

    def block(kind, i):
        slot, slots, chunk, chunks = PIECES[kind][i]
        put(kind, i, forces(kind * 256 + 32 * chunk, 32 * chunks, 128 * slot, 128 * slots))

    def take_a(i):
        a_copy(i).wait()
        split_a(a_rem, REM, *A_SENT[i])

    def take_b(i):
        b_copy(i).wait()
        split_b(b_rem, REM, *B_SENT[i])

    for i in range(max(len(A_SENT), len(B_SENT))):
        if i < len(A_SENT):
            a_copy(i).start()
        if i < len(B_SENT):
            b_copy(i).start()

    for load in loads:
        load.wait()
    for t in range(CHUNKS):
        split_a(a_own, OWN, t, 0, TWELFTHS)
        split_b(b_own, OWN, 32 * t, 32, 0, TWELFTHS)
    block(OWN, 0)

    for i in range(4):
        take_a(i)
        take_b(i)
        if i == 0:
            forward(OWN, 0)
    block(REM, 0)
    block(OWN, 1)
    take_a(4)
    take_b(4)
    forward(REM, 0)
    forward(OWN, 1)
    take_a(5)
    take_b(5)
    block(REM, 1)
    take_a(6)
    take_b(6)
    forward(REM, 1)
    block(REM, 2)
    last_panel[pl.ds(0, 480)] = forces(0, 480, 384, 128, 0, 9)
    take_a(7)
    forward(REM, 2)
    value = forces(480, 32, 0, 512, 0, 6)
    last_rows[...] = value[:, :384]
    last_panel[pl.ds(480, 32)] = value[:, 384:]
    take_b(7)
    last_panel[pl.ds(0, 480)] += forces(0, 480, 384, 128, 9, 2)
    take_a(8)
    value = forces(480, 32, 0, 512, 6, 3)
    last_rows[...] += value[:, :384]
    last_panel[pl.ds(480, 32)] += value[:, 384:]
    take_a(9)
    value = forces(480, 32, 0, 512, 9, 2)
    last_rows[...] += value[:, :384]
    last_panel[pl.ds(480, 32)] += value[:, 384:]
    take_b(8)
    put(OWN, 2, last_panel[pl.ds(0, 256)] + forces(0, 256, 384, 128, 11, 1))
    take_a(10)
    put(REM, 4, last_panel[pl.ds(256, 256)] + forces(256, 256, 384, 128, 11, 1))
    put(REM, 3, last_rows[...] + forces(480, 32, 0, 384, 11, 1))
    forward(OWN, 2)
    forward(REM, 4)
    forward(REM, 3)

    mine = (d // 4 + x) % 2
    for kind in (OWN, REM):
        @pl.when(mine == kind)
        def _():
            for i, (slot, slots, chunk, chunks) in enumerate(PIECES[kind]):
                for o in range(1, 4):
                    other = (z + o) % 4
                    landed = parts.at[other, pl.ds(slot, slots), pl.ds(chunk, chunks)]
                    pltpu.make_async_copy(landed, landed, r_recv.at[i, other]).wait()

    total = chip[mine, z % 2]
    for o in range(1, 4):
        total = total + parts[(z + o) % 4]
    red[...] = total

    def plane_copy(o):
        peer = (p + o) % 4
        return pltpu.make_async_remote_copy(
            src_ref=red.at[:, pl.ds(2 * peer, 2)], dst_ref=plane.at[pl.ds(4 * p, 4)],
            send_sem=p_send.at[o], recv_sem=p_recv.at[p],
            device_id={"phase": peer, "slab": d}, device_id_type=MESH,
        )

    for o in range(1, 4):
        plane_copy(o).start()
    plane[pl.ds(4 * p, 4)] = red[:, pl.ds(2 * p, 2)]
    for o in range(1, 4):
        other = (p + o) % 4
        landed = plane.at[pl.ds(4 * other, 4)]
        pltpu.make_async_copy(landed, landed, p_recv.at[other]).wait()

    def panel(half, peer):
        q = order_ref[peer]
        off = q // 4 - half
        return plane[(half * 2 + q // 2 % 2) * 4 + off * off * 2 + q % 2]

    def slab_copy(o):
        peer = (d + o) % SLABS
        return pltpu.make_async_remote_copy(
            src_ref=picked.at[o], dst_ref=gathered.at[d],
            send_sem=g_send.at[o], recv_sem=g_recv.at[d],
            device_id={"phase": p, "slab": peer}, device_id_type=MESH,
        )

    for o in range(1, SLABS):
        for half in range(2):
            picked[o, half] = panel(half, (d + o) % SLABS)
        slab_copy(o).start()
    for half in range(2):
        gathered[d, half] = panel(half, d)
    for o in range(1, SLABS):
        other = (d + o) % SLABS
        landed = gathered.at[other]
        pltpu.make_async_copy(landed, landed, g_recv.at[other]).wait()

    for kind in (OWN, REM):
        for i in range(len(PIECES[kind])):
            for h in range(2):
                peer_copy(kind, i, h, lambda copy: copy.wait_send())
    for o in range(1, 4):
        plane_copy(o).wait_send()
    for o in range(1, SLABS):
        slab_copy(o).wait_send()


def blade_kernel(gathered, out_ref):
    blades = 16
    scale = 1.0 / math.sqrt(blades)
    cosine = [round(math.cos(2 * math.pi * i / blades), 15) * scale for i in range(blades)]
    sine = [round(math.sin(2 * math.pi * i / blades), 15) * scale for i in range(blades)]
    for b in range(blades):
        real, imag = None, None
        for k in range(blades):
            c, s = cosine[k * b % blades], sine[k * b % blades]
            re, im = gathered[k % 8, k // 8, 0], gathered[k % 8, k // 8, 1]
            terms = [(re * c, im * c)] if c else []
            if s:
                terms.append((im * -s, re * s))
            for first, second in terms:
                real = first if real is None else real + first
                imag = second if imag is None else imag + second
        out_ref[0, b] = real
        out_ref[1, b] = imag


def fused(pressure, mode_shapes, point_weight, panel_order):
    points = pressure.shape[3]
    vmem = pltpu.VMEM
    dma = pltpu.SemaphoreType.DMA
    gathered = pl.pallas_call(
        kernel,
        out_shape=jax.ShapeDtypeStruct((8, 2, 2, 8, 128), F32),
        in_specs=[
            pl.BlockSpec(memory_space=pltpu.SMEM),
            pl.BlockSpec(memory_space=pl.ANY),
            pl.BlockSpec(memory_space=pl.ANY),
            pl.BlockSpec(memory_space=pltpu.VMEM),
        ],
        out_specs=pl.BlockSpec(memory_space=pltpu.VMEM),
        scratch_shapes=[
            vmem((CHUNKS, 4, 8, points), F32),
            vmem((256, points), F32),
            vmem((CHUNKS, 4, 8, points), F32),
            vmem((256, points), F32),
            vmem((512, points), BF16),
            vmem((512, points), BF16),
            vmem((512, points), BF16),
            vmem((512, points), BF16),
            vmem((2, 2, 2, 4, CHUNKS, 8, 128), F32),
            vmem((2, 2, 4, CHUNKS, 8, 128), F32),
            vmem((2, 2, 4, CHUNKS, 8, 128), F32),
            vmem((4, 4, CHUNKS, 8, 128), F32),
            vmem((4, CHUNKS, 8, 128), F32),
            vmem((16, 2, 8, 128), F32),
            vmem((8, 2, 2, 8, 128), F32),
            vmem((512, 128), F32),
            vmem((32, 384), F32),
            dma((CHUNKS + 1,)),
            dma((len(A_SENT),)), dma((len(A_SENT),)), dma((len(B_SENT),)), dma((len(B_SENT),)),
            dma((2, 5)), dma((2, 5)),
            dma((2, 5, 2)), dma((5, 4)),
            dma((4,)), dma((4,)),
            dma((8,)), dma((8,)),
        ],
        compiler_params=pltpu.CompilerParams(
            collective_id=0, has_side_effects=True, vmem_limit_bytes=56 * 1024 * 1024
        ),
        cost_estimate=pl.CostEstimate(
            flops=6 * 512 * 512 * points, bytes_accessed=16 * 256 * points, transcendentals=0
        ),
    )(panel_order, pressure, mode_shapes, point_weight.reshape(1, points))
    return pl.pallas_call(
        blade_kernel, out_shape=jax.ShapeDtypeStruct((2, 16, 8, 128), F32),
    )(gathered)


def solution(mesh):
    def shards(pressure, mode_shapes, point_weight, panel_order):
        fits = (
            mesh.shape["phase"] == 4
            and mesh.shape["slab"] == SLABS
            and pressure.shape[:3] == (2, 4, 32)
            and pressure.shape[3] % 1536 == 0
            and pressure.shape[3] <= 3072
            and mode_shapes.shape[0] == 256
            and panel_order.shape[0] == 8
        )
        body = fused if fits else general
        return body(pressure, mode_shapes, point_weight, panel_order)

    placed = (P(None, "phase", None, "slab"), P("phase", "slab"), P("slab"), P())
    return jax.shard_map(
        shards,
        mesh=mesh,
        in_specs=placed,
        out_specs=P(None, None, "phase", "slab"),
        check_vma=False,
    )
```
